768 devices in a mesh: wide: 96 (over y, z), narrow: 8 (over x, core).
Axes of the slice: x: 4, y: 8, z: 12, core: 2. Of those that a mesh axis runs over, the one named last changes fastest.
Arguments:
- tile_values: bfloat16 [98304, 128, 128], P(('wide', 'narrow')), may hold values from -6 to 6
- tile_row: int32 [98304], P(('wide', 'narrow')), may hold values from 0 to 15
- tile_col: int32 [98304], P(('wide', 'narrow')), may hold values from 0 to 23
- tile_count: int32 [768], P(('wide', 'narrow')), may hold values from 32 to 128, as said below
- user_degree: int32 [196608], P('wide'), may hold values from 16 to 3968
- item_degree: int32 [24576], P('narrow'), may hold values from 16 to 3968
- start_vectors: float32 [64, 24576], P(None, 'narrow'), may hold values from -6 to 6
Outputs:
- user_vectors: float32 [64, 196608], P(None, 'wide')
- item_vectors: float32 [64, 24576], P(None, 'narrow')
The draws below stay inside these ranges and needn't reach their ends.
Inputs may be any that keep to these rules, and one draw needn't show every extreme that they name: `tile_count`: each device's used slots are its first ones; some device uses all 128.
All inputs are finite; a program needn't handle non-finite values.
Results may differ from the reference program's by a relative error of at most 0.0041.
Values sent between devices are 32-bit elements; how exact they have to be, the bound alone decides.
No kernel may reach another device: no remote copies, remote signals or barrier semaphores. Data moves between devices by JAX's collectives and lax.ppermute only.
A program may use at most 32 MiB of HBM per device.

```python
import jax
import jax.numpy as jnp
from jax import lax

TILE = 128
VECTORS = 64
ITERS = 2
TILES_DEV = 128
UB_DEV = 16
IB_DEV = 24
U_DEV = 2048
I_DEV = 3072
USERS = 196608
ITEMS = 24576
OWNERS = 768
TILES = 98304
N_WIDE = 96
N_NARROW = 8


def spread_degree(key, count):
    first_key, second_key = jax.random.split(key)
    leading = jax.random.randint(first_key, (count,), 16, 32, dtype=jnp.int32)
    powers = jax.random.randint(second_key, (count,), 0, 8, dtype=jnp.int32)
    return jnp.left_shift(leading, powers).astype(jnp.int32)


def draw_user_degree(key, part):
    key = jax.random.fold_in(key, 1)
    return spread_degree(key, USERS)


def draw_item_degree(key, part):
    key = jax.random.fold_in(key, 2)
    return spread_degree(key, ITEMS)


def draw_tile_count(key, part):
    key = jax.random.fold_in(key, 3)
    first_key, second_key, third_key = jax.random.split(key, 3)
    lowest = max(1, TILES_DEV // 4)
    base = jax.random.randint(first_key, (OWNERS,), lowest, max(lowest, TILES_DEV // 2) + 1, dtype=jnp.int32)
    filled = jax.random.randint(second_key, (OWNERS,), 0, 8, dtype=jnp.int32) == 0
    chosen = jax.random.randint(third_key, (), 0, OWNERS, dtype=jnp.int32)
    counts = jnp.where(filled, TILES_DEV, base)
    counts = jnp.where(jnp.arange(OWNERS, dtype=jnp.int32) == chosen, TILES_DEV, counts)
    return counts.astype(jnp.int32)


def touch_ends(entries, stream_key, low, top_value):
    dims = entries.shape
    place = [jax.random.randint(jax.random.fold_in(stream_key, axis), (), 0, dims[axis]) for axis in range(len(dims))]
    entries = entries.at[tuple(place)].set(low)
    longest = dims.index(max(dims))
    place[longest] = (place[longest] + 1) % dims[longest]
    return entries.at[tuple(place)].set(top_value)


def block_levels(stream_key, dims, shards, smallest, largest):
    loudness, own = 1.0, jax.random.fold_in(stream_key, 6)
    for axis_at, shards_of in shards:
        heights = jnp.exp(jax.random.uniform(jax.random.fold_in(own, axis_at), (shards_of,), jnp.float32, smallest / len(shards), largest / len(shards)))
        loudness = loudness * jnp.repeat(heights, dims[axis_at] // shards_of).reshape([-1 if axis == axis_at else 1 for axis in range(len(dims))])
    return loudness


def bell_draw(own_key, dims, width, most, shards=(), held_as=jnp.bfloat16):
    array = jax.random.normal(own_key, dims, jnp.float32) * width
    if len(shards) > 0:
        array = block_levels(own_key, dims, shards, -0.22, 0.18) * array
    return jnp.clip(array, min=-most, max=most).astype(held_as)


def setup_inputs(seed: int = 0) -> dict:
    key_list = jax.random.split(jax.random.key(seed), 8)
    return {
        "tile_values": bell_draw(key_list[0], (TILES, TILE, TILE), 1.0, 6.0, ((0, 768),)),
        "tile_row": touch_ends(jax.random.randint(key_list[1], (TILES,), 0, UB_DEV), jax.random.fold_in(key_list[1], 1), 0, UB_DEV - 1).astype(jnp.int32),
        "tile_col": touch_ends(jax.random.randint(key_list[2], (TILES,), 0, IB_DEV), jax.random.fold_in(key_list[2], 1), 0, IB_DEV - 1).astype(jnp.int32),
        "tile_count": draw_tile_count(jax.random.fold_in(key_list[7], 71), 0),
        "user_degree": draw_user_degree(jax.random.fold_in(key_list[7], 71), 0),
        "item_degree": draw_item_degree(jax.random.fold_in(key_list[7], 71), 0),
        "start_vectors": bell_draw(key_list[6], (VECTORS, ITEMS), 1.0, 6.0, ((1, 8),), jnp.float32),
    }


def reference(tile_values, tile_row, tile_col, tile_count, user_degree, item_degree, start_vectors):
    item_blocks = I_DEV // TILE
    user_blocks = U_DEV // TILE
    all_blocks = ITEMS // TILE
    user_scale = lax.rsqrt(user_degree.astype(jnp.float32))
    item_scale = lax.rsqrt(item_degree.astype(jnp.float32))
    tiles_by_wide = tile_values.reshape(N_WIDE, N_NARROW * TILES_DEV, TILE, TILE)
    rows_by_wide = tile_row.reshape(N_WIDE, N_NARROW * TILES_DEV)
    column_offset = (jnp.arange(N_NARROW, dtype=jnp.int32) * item_blocks).astype(jnp.int32)
    cols_by_wide = (tile_col.reshape(N_WIDE, N_NARROW, TILES_DEV) + column_offset[None, :, None]).astype(jnp.int32)
    cols_by_wide = cols_by_wide.reshape(N_WIDE, N_NARROW * TILES_DEV)
    slot_index = jnp.arange(TILES_DEV, dtype=jnp.int32)
    in_use = (slot_index[None, None, :] < tile_count.reshape(N_WIDE, N_NARROW)[:, :, None]).astype(jnp.float32)
    in_use = in_use.reshape(N_WIDE, N_NARROW * TILES_DEV)
    item_vectors = start_vectors
    user_vectors = None
    for step in range(ITERS):
        scaled_items = (item_vectors * item_scale[None, :]).astype(jnp.bfloat16)
        item_source = scaled_items.reshape(VECTORS, all_blocks, TILE)

        def forward_block(pieces):
            tiles_here, rows_here, cols_here, use_here = pieces
            picked = jnp.take(item_source, cols_here, axis=1).astype(jnp.float32)
            products = jnp.einsum('ktc,trc->ktr', picked, tiles_here.astype(jnp.float32))
            products = products * use_here[None, :, None]
            summed = jnp.zeros((VECTORS, user_blocks, TILE), jnp.float32).at[:, rows_here].add(products)
            return summed.reshape(VECTORS, U_DEV)
        user_sums = lax.map(forward_block, (tiles_by_wide, rows_by_wide, cols_by_wide, in_use))
        user_sums = jnp.transpose(user_sums, (1, 0, 2)).reshape(VECTORS, USERS)
        user_raw = user_sums * user_scale[None, :]
        user_gram = jnp.dot(user_raw, user_raw.T, precision=lax.Precision.HIGHEST) / USERS
        factor = jnp.linalg.cholesky(user_gram)
        user_vectors = jax.scipy.linalg.solve_triangular(factor, user_raw, lower=True)
        scaled_users = (user_vectors * user_scale[None, :]).astype(jnp.bfloat16)
        user_source = jnp.transpose(scaled_users.reshape(VECTORS, N_WIDE, user_blocks, TILE), (1, 0, 2, 3))

        def backward_block(carry, pieces):
            tiles_here, rows_here, cols_here, use_here, users_here = pieces
            picked = jnp.take(users_here, rows_here, axis=1).astype(jnp.float32)
            products = jnp.einsum('ktr,trc->ktc', picked, tiles_here.astype(jnp.float32))
            products = products * use_here[None, :, None]
            return (carry.at[:, cols_here].add(products), None)
        start_carry = jnp.zeros((VECTORS, all_blocks, TILE), jnp.float32)
        item_sums, unused = lax.scan(backward_block, start_carry, (tiles_by_wide, rows_by_wide, cols_by_wide, in_use, user_source))
        item_raw = item_sums.reshape(VECTORS, ITEMS) * item_scale[None, :]
        item_gram = jnp.dot(item_raw, item_raw.T, precision=lax.Precision.HIGHEST) / ITEMS
        factor_two = jnp.linalg.cholesky(item_gram)
        item_vectors = jax.scipy.linalg.solve_triangular(factor_two, item_raw, lower=True)
    return (user_vectors, item_vectors)
```

```python
import jax
import jax.numpy as jnp
from jax import lax
from jax.experimental import pallas as pl
from jax.experimental.pallas import tpu as pltpu
from jax.sharding import PartitionSpec as P

ITERS = 2
GROUP = 16


def product_body(forward, blocks_out, vectors, src_ref, dst_ref, x_ref, tiles_ref, out_ref):
    step = pl.program_id(0)

    @pl.when(step == 0)
    def _():
        out_ref[...] = jnp.zeros_like(out_ref)

    terms = x_ref.shape[1] // vectors
    dims = (((1,), (1,)), ((), ())) if forward else (((1,), (0,)), ((), ()))
    for slot in range(GROUP):
        at = step * GROUP + slot
        product = lax.dot_general(
            x_ref[src_ref[at]], tiles_ref[slot], dims, preferred_element_type=jnp.float32
        )
        total = product[:vectors]
        for term in range(1, terms):
            total = total + product[term * vectors : (term + 1) * vectors]
        out_ref[dst_ref[at]] += total


def products(x, tiles, src, dst, blocks_out, vectors, forward):
    slots, tile, _ = tiles.shape
    blocks_in, rows, _ = x.shape

    def body(*refs):
        product_body(forward, blocks_out, vectors, *refs)

    out = pl.pallas_call(
        body,
        grid_spec=pltpu.PrefetchScalarGridSpec(
            num_scalar_prefetch=2,
            grid=(slots // GROUP,),
            in_specs=[
                pl.BlockSpec((blocks_in, rows, tile), lambda i, *_: (0, 0, 0)),
                pl.BlockSpec((GROUP, tile, tile), lambda i, *_: (i, 0, 0)),
            ],
            out_specs=pl.BlockSpec((blocks_out + 1, vectors, tile), lambda i, *_: (0, 0, 0)),
        ),
        out_shape=jax.ShapeDtypeStruct((blocks_out + 1, vectors, tile), jnp.float32),
        compiler_params=pltpu.CompilerParams(vmem_limit_bytes=32 * 1024 * 1024),
        name="products",
    )(src, dst, x, tiles)
    return out[:blocks_out]


def split_terms(x):
    high = x.astype(jnp.bfloat16)
    low = (x - high.astype(jnp.float32)).astype(jnp.bfloat16)
    return jnp.concatenate([high, low], axis=1)


def gram_of(raw):
    return jnp.einsum("bkc,bjc->kj", raw, raw, precision=lax.Precision.HIGHEST)


def inverse_factor(gram):
    factor = jnp.linalg.cholesky(gram)
    eye = jnp.eye(gram.shape[0], dtype=gram.dtype)
    return jax.scipy.linalg.solve_triangular(factor, eye, lower=True)


def apply_left(inverse, raw):
    return jnp.einsum("kj,bjc->bkc", inverse, raw, precision=lax.Precision.HIGHEST)


def sum_over(chunks, axis):
    got = lax.all_to_all(chunks, axis, 0, 0)
    mine = jnp.sum(got, axis=0, keepdims=True)
    copies = jnp.broadcast_to(mine, chunks.shape)
    return lax.all_to_all(copies, axis, 0, 0)


def local(tile_values, tile_row, tile_col, tile_count, user_degree, item_degree, start_vectors):
    vectors, item_rows = start_vectors.shape
    slot_count, tile, _ = tile_values.shape
    user_rows = user_degree.shape[0]
    user_blocks = user_rows // tile
    item_blocks = item_rows // tile
    wide_count = lax.axis_size("wide")
    narrow_count = lax.axis_size("narrow")
    all_users = user_rows * wide_count
    all_items = item_rows * narrow_count
    user_scale = lax.rsqrt(user_degree.astype(jnp.float32)).reshape(user_blocks, 1, tile)
    item_scale = lax.rsqrt(item_degree.astype(jnp.float32)).reshape(item_blocks, 1, tile)
    used = jnp.arange(slot_count, dtype=jnp.int32) < tile_count[0]
    row_out = jnp.where(used, tile_row, user_blocks)
    col_out = jnp.where(used, tile_col, item_blocks)

    def narrow_sum(terms, gram):
        data = terms.reshape(narrow_count, -1, tile)
        count = data.shape[1]
        if gram is None:
            return sum_over(data, "narrow").reshape(terms.shape), None
        wide_gram = jnp.pad(gram, ((0, 0), (0, tile - vectors))).reshape(narrow_count, -1, tile)
        both = sum_over(jnp.concatenate([data, wide_gram], axis=1), "narrow")
        return both[:, :count].reshape(terms.shape), both[:, count:].reshape(vectors, tile)[:, :vectors]

    def wide_sum(terms, gram):
        data = terms.reshape(wide_count, 1, -1)
        count = data.shape[2]
        wide_gram = jnp.pad(gram, ((0, wide_count - vectors), (0, tile - vectors))).reshape(wide_count, 1, tile)
        both = sum_over(jnp.concatenate([data, wide_gram], axis=2), "wide")
        return both[:, :, :count].reshape(terms.shape), both[:, 0, count:][:vectors, :vectors]

    start = jnp.transpose(start_vectors.reshape(vectors, item_blocks, tile), (1, 0, 2))
    item_source = (start * item_scale).astype(jnp.bfloat16)
    item_gram = None
    for step in range(ITERS):
        user_terms = products(item_source, tile_values, tile_col, row_out, user_blocks, vectors, True)
        user_sums, item_gram = narrow_sum(user_terms, item_gram)
        user_raw = user_sums * user_scale
        if item_gram is not None:
            user_raw = apply_left(inverse_factor(item_gram / all_items), user_raw)
        user_gram = gram_of(user_raw)
        user_source = split_terms(user_raw * user_scale)
        item_terms = products(user_source, tile_values, tile_row, col_out, item_blocks, vectors, False)
        item_sums, user_gram = wide_sum(item_terms, user_gram)
        user_inverse = inverse_factor(user_gram / all_users)
        item_raw = apply_left(user_inverse, item_sums) * item_scale
        item_gram = gram_of(item_raw)
        item_source = split_terms(item_raw * item_scale)
    copies = jnp.broadcast_to(item_gram[None], (narrow_count, vectors, vectors))
    item_gram = jnp.sum(lax.all_to_all(copies, "narrow", 0, 0), axis=0)
    item_inverse = inverse_factor(item_gram / all_items)
    user_vectors = jnp.einsum("kj,bjc->kbc", user_inverse, user_raw, precision=lax.Precision.HIGHEST)
    item_vectors = jnp.einsum("kj,bjc->kbc", item_inverse, item_raw, precision=lax.Precision.HIGHEST)
    return (user_vectors.reshape(vectors, user_rows), item_vectors.reshape(vectors, item_rows))


def solution(mesh):
    return jax.shard_map(
        local,
        mesh=mesh,
        in_specs=(
            P(("wide", "narrow"), None, None),
            P(("wide", "narrow")),
            P(("wide", "narrow")),
            P(("wide", "narrow")),
            P("wide"),
            P("narrow"),
            P(None, "narrow"),
        ),
        out_specs=(P(None, "wide"), P(None, "narrow")),
        check_vma=False,
    )
```

```python
import jax
import jax.numpy as jnp
from jax import lax
from jax.experimental import pallas as pl
from jax.experimental.pallas import tpu as pltpu
from jax.sharding import Mesh, PartitionSpec as P

ITERS = 2
GROUP = 16
Y_CHIPS = 8
SUB = 8
FULL = lax.Precision.HIGHEST
VMEM = pl.BlockSpec(memory_space=pltpu.VMEM)


def dot(a, b, last=False):
    dims = (((1,), (1,)), ((), ())) if last else (((1,), (0,)), ((), ()))
    return lax.dot_general(a, b, dims, precision=FULL, preferred_element_type=jnp.float32)


def inverse_factor(panels):
    vectors = len(panels) * SUB
    lane = lax.broadcasted_iota(jnp.int32, (SUB, 2 * vectors), 1)
    sub = lax.broadcasted_iota(jnp.int32, (SUB, 2 * vectors), 0)
    rows = []
    for p, panel in enumerate(panels):
        unit = jnp.where(lane == vectors + p * SUB + sub, 1.0, 0.0)
        rows.append(jnp.where(lane < vectors, panel, unit))

    def spread(panel, p):
        return [jnp.broadcast_to(panel[:, p * SUB + q : p * SUB + q + 1], panel.shape) for q in range(SUB)]

    def row(value, q):
        return jnp.broadcast_to(value[q : q + 1, :], value.shape)

    for p in range(len(panels)):
        cols = spread(rows[p], p)
        pivots, heads, inverses = [], [], []
        scale = jnp.ones_like(rows[p])
        for q in range(SUB):
            head = row(rows[p], q)
            tops = [None if t < q else row(cols[t], q) for t in range(SUB)]
            inverse = 1.0 / tops[q]
            pivots.append(head)
            heads.append(tops)
            inverses.append(inverse)
            scale = jnp.where(sub == q, tops[q], scale)
            factor = jnp.where(sub > q, cols[q] * inverse, 0.0)
            rows[p] = rows[p] - factor * head
            for t in range(q + 1, SUB):
                cols[t] = cols[t] - factor * tops[t]
        for r in range(p + 1, len(panels)):
            cols = spread(rows[r], p)
            for q in range(SUB):
                factor = cols[q] * inverses[q]
                rows[r] = rows[r] - factor * pivots[q]
                for t in range(q + 1, SUB):
                    cols[t] = cols[t] - factor * heads[q][t]
        rows[p] = rows[p] * lax.rsqrt(scale)
    return jnp.concatenate(rows, axis=0)[:, vectors:]


def padded(gram):
    return jnp.concatenate([gram, jnp.zeros_like(gram)], axis=1)


def phase(data, scale, tiles, src, dst, blocks_out, forward, gram_count, round_first, send_gram, keep_raw):
    slots, tile, _ = tiles.shape
    blocks, _, _ = scale.shape
    chunks = data.shape[0]
    vectors = tile // 2
    per_chunk = blocks // chunks
    have_gram = gram_count is not None
    terms = 1 if round_first else 2
    out_chunks = Y_CHIPS
    out_per = blocks_out // out_chunks
    out_rows = out_per * vectors + (SUB if send_gram else 0)
    steps = slots // GROUP
    dims = (((1,), (1,)), ((), ())) if forward else (((1,), (0,)), ((), ()))

    def body(src_ref, dst_ref, data_ref, scale_ref, tiles_ref, out_ref, *rest):
        if keep_raw:
            raw_ref, x_ref, sums_ref, gram_ref = rest
        else:
            x_ref, sums_ref, gram_ref = rest
        step = pl.program_id(0)

        @pl.when(step == 0)
        def _():
            sums_ref[...] = jnp.zeros_like(sums_ref)
            inverse = None
            if have_gram:
                at = per_chunk * vectors
                inverse = inverse_factor([data_ref[c, at : at + SUB, :] * (1.0 / gram_count) for c in range(chunks)])
            gram = jnp.zeros((vectors, vectors), jnp.float32)
            for block in range(blocks):
                at = (block % per_chunk) * vectors
                raw = data_ref[block // per_chunk, at : at + vectors, :]
                weight = scale_ref[block]
                if not round_first:
                    if have_gram:
                        raw = dot(inverse, raw)
                    raw = raw * weight
                if keep_raw:
                    raw_ref[block] = raw
                if send_gram:
                    gram = gram + dot(raw, raw, last=True)
                source = raw * weight
                high = source.astype(jnp.bfloat16)
                x_ref[block, :vectors, :] = high
                if terms == 2:
                    x_ref[block, vectors:, :] = (source - high.astype(jnp.float32)).astype(jnp.bfloat16)
            if send_gram:
                gram_ref[...] = padded(gram)

        for slot in range(GROUP):
            at = step * GROUP + slot
            product = lax.dot_general(
                x_ref[src_ref[at]], tiles_ref[slot], dims, preferred_element_type=jnp.float32
            )
            if terms == 2:
                product = product[:vectors] + product[vectors:]
            sums_ref[dst_ref[at]] += product

        @pl.when(step == steps - 1)
        def _():
            for block in range(blocks_out):
                at = (block % out_per) * vectors
                out_ref[block // out_per, at : at + vectors, :] = sums_ref[block]
            if send_gram:
                for c in range(out_chunks):
                    out_ref[c, out_per * vectors :, :] = gram_ref[c * SUB : (c + 1) * SUB, :]

    out_shape = [jax.ShapeDtypeStruct((out_chunks, out_rows, tile), jnp.float32)]
    out_specs = [pl.BlockSpec((out_chunks, out_rows, tile), lambda i, *_: (0, 0, 0))]
    if keep_raw:
        out_shape.append(jax.ShapeDtypeStruct((blocks, vectors, tile), jnp.float32))
        out_specs.append(pl.BlockSpec((blocks, vectors, tile), lambda i, *_: (0, 0, 0)))
    return pl.pallas_call(
        body,
        grid_spec=pltpu.PrefetchScalarGridSpec(
            num_scalar_prefetch=2,
            grid=(steps,),
            in_specs=[
                pl.BlockSpec(data.shape, lambda i, *_: (0, 0, 0)),
                pl.BlockSpec(scale.shape, lambda i, *_: (0, 0, 0)),
                pl.BlockSpec((GROUP, tile, tile), lambda i, *_: (i, 0, 0)),
            ],
            out_specs=out_specs,
            scratch_shapes=[
                pltpu.VMEM((blocks, terms * vectors, tile), jnp.bfloat16),
                pltpu.VMEM((blocks_out + 1, vectors, tile), jnp.float32),
                pltpu.VMEM((vectors, tile), jnp.float32),
            ],
        ),
        out_shape=out_shape,
        compiler_params=pltpu.CompilerParams(vmem_limit_bytes=VMEM_LIMIT),
        name="forward" if forward else "backward",
    )(src, dst, data, scale, tiles)


VMEM_LIMIT = 32 * 1024 * 1024


def call(body, inputs, shapes, name):
    return pl.pallas_call(
        body,
        in_specs=[VMEM] * len(inputs),
        out_specs=[VMEM] * len(shapes),
        out_shape=[jax.ShapeDtypeStruct(s, jnp.float32) for s in shapes],
        compiler_params=pltpu.CompilerParams(vmem_limit_bytes=VMEM_LIMIT),
        name=name,
    )(*inputs)


def total(ref, begin, end):
    value = ref[0, begin:end, :]
    for c in range(1, ref.shape[0]):
        value = value + ref[c, begin:end, :]
    return value


def exchange(data, axis):
    return lax.all_to_all(data, axis, 0, 0)


def narrow_sum(chunks):
    def body(got_ref, out_ref):
        mine = total(got_ref, 0, got_ref.shape[1])
        for c in range(out_ref.shape[0]):
            out_ref[c] = mine

    (copies,) = call(body, [exchange(chunks, "narrow")], [chunks.shape], "sum_copies")
    return exchange(copies, "narrow")


def wide_sum(chunks, z_count):
    rows, tile = chunks.shape[1] - SUB, chunks.shape[2]
    part = rows // z_count

    def split(got_ref, out_ref):
        last = total(got_ref, rows, rows + SUB)
        for c in range(z_count):
            out_ref[c, :part, :] = total(got_ref, c * part, (c + 1) * part)
            out_ref[c, part:, :] = last

    def spread(got_ref, out_ref, last_ref):
        mine = total(got_ref, 0, part)
        for c in range(z_count):
            out_ref[c] = mine
        last_ref[...] = total(got_ref, part, part + SUB)

    def copies(got_ref, last_ref, out_ref):
        for c in range(out_ref.shape[0]):
            for z in range(z_count):
                out_ref[c, z * part : (z + 1) * part, :] = got_ref[z]
            out_ref[c, rows:, :] = last_ref[...]

    (parts,) = call(split, [exchange(chunks, "y")], [(z_count, part + SUB, tile)], "sum_split")
    mine, last = call(spread, [exchange(parts, "z")], [(z_count, part, tile), (SUB, tile)], "sum_spread")
    (back,) = call(copies, [exchange(mine, "z"), last], [chunks.shape], "copies")
    return exchange(back, "y")


def finish_items(data, scale, user_count):
    chunks, rows, tile = data.shape
    blocks = scale.shape[0]
    vectors = tile // 2
    per_chunk = blocks // chunks

    def body(data_ref, scale_ref, raw_ref, gram_ref, inverse_ref):
        at = per_chunk * vectors
        inverse = inverse_factor([data_ref[c, at : at + SUB, :] * (1.0 / user_count) for c in range(chunks)])
        inverse_ref[...] = inverse
        gram = jnp.zeros((vectors, vectors), jnp.float32)
        for block in range(blocks):
            at = (block % per_chunk) * vectors
            raw = dot(inverse, data_ref[block // per_chunk, at : at + vectors, :]) * scale_ref[block]
            raw_ref[block] = raw
            gram = gram + dot(raw, raw, last=True)
        packed = jnp.concatenate([gram[: vectors // 2], gram[vectors // 2 :]], axis=1)
        for c in range(gram_ref.shape[0]):
            gram_ref[c] = packed

    shapes = [(blocks, vectors, tile), (Y_CHIPS, vectors // 2, tile), (vectors, vectors)]
    return call(body, [data, scale], shapes, "finish_items")


def finish_users(raw, inverse):
    blocks, vectors, tile = raw.shape

    def body(raw_ref, inverse_ref, out_ref):
        for block in range(blocks):
            out_ref[:, block * tile : (block + 1) * tile] = dot(inverse_ref[...], raw_ref[block])

    return call(body, [raw, inverse], [(vectors, blocks * tile)], "finish_users")[0]


def finish_vectors(raw, grams, item_count):
    blocks, vectors, tile = raw.shape

    def body(raw_ref, grams_ref, out_ref):
        gram = total(grams_ref, 0, vectors // 2) * (1.0 / item_count)
        gram = jnp.concatenate([gram[:, :vectors], gram[:, vectors:]], axis=0)
        gram = padded(gram)
        inverse = inverse_factor([gram[at : at + SUB] for at in range(0, vectors, SUB)])
        for block in range(blocks):
            out_ref[:, block * tile : (block + 1) * tile] = dot(inverse, raw_ref[block])

    return call(body, [raw, grams], [(vectors, blocks * tile)], "finish_vectors")[0]


def local(tile_values, tile_row, tile_col, tile_count, user_degree, item_degree, start_vectors):
    vectors, item_rows = start_vectors.shape
    slot_count, tile, _ = tile_values.shape
    user_rows = user_degree.shape[0]
    user_blocks = user_rows // tile
    item_blocks = item_rows // tile
    z_count = lax.axis_size("z")
    all_users = user_rows * lax.axis_size("y") * z_count
    all_items = item_rows * lax.axis_size("narrow")
    user_scale = lax.rsqrt(user_degree.astype(jnp.float32)).reshape(user_blocks, 1, tile)
    item_scale = lax.rsqrt(item_degree.astype(jnp.float32)).reshape(item_blocks, 1, tile)
    used = jnp.arange(slot_count, dtype=jnp.int32) < tile_count[0]
    row_out = jnp.where(used, tile_row, user_blocks)
    col_out = jnp.where(used, tile_col, item_blocks)

    item_data = jnp.transpose(start_vectors.reshape(vectors, item_blocks, tile), (1, 0, 2))
    for step in range(ITERS):
        first, last = step == 0, step == ITERS - 1
        (terms,) = phase(
            item_data, item_scale, tile_values, tile_col, row_out, user_blocks, True,
            None if first else all_users, first, not first, False,
        )
        user_data = narrow_sum(terms)
        out = phase(
            user_data, user_scale, tile_values, tile_row, col_out, item_blocks, False,
            None if first else all_items, False, True, last,
        )
        item_data = wide_sum(out[0], z_count)
    user_raw = out[1]
    item_raw, grams, user_inverse = finish_items(item_data, item_scale, all_users)
    grams = exchange(grams, "narrow")
    user_vectors = finish_users(user_raw, user_inverse)
    item_vectors = finish_vectors(item_raw, grams, all_items)
    return (user_vectors, item_vectors)


def solution(mesh):
    wide_count, narrow_count = mesh.devices.shape
    grid = mesh.devices.reshape(Y_CHIPS, wide_count // Y_CHIPS, narrow_count)
    owner = ("y", "z", "narrow")
    return jax.shard_map(
        local,
        mesh=Mesh(grid, owner),
        in_specs=(
            P(owner, None, None),
            P(owner),
            P(owner),
            P(owner),
            P(("y", "z")),
            P("narrow"),
            P(None, "narrow"),
        ),
        out_specs=(P(None, ("y", "z")), P(None, "narrow")),
        check_vma=False,
    )
```

```python
import math

import jax
import jax.numpy as jnp
from jax import lax
from jax.experimental import pallas as pl
from jax.experimental.pallas import tpu as pltpu
from jax.sharding import Mesh, PartitionSpec as P

ITERS = 2
GROUP = 16
Y_CHIPS = 8
Z_PAIR = 2
SUB = 8
WIDTH = 4
FULL = lax.Precision.HIGHEST
VMEM = pl.BlockSpec(memory_space=pltpu.VMEM)


def dot(a, b, last=False):
    dims = (((1,), (1,)), ((), ())) if last else (((1,), (0,)), ((), ()))
    return lax.dot_general(a, b, dims, precision=FULL, preferred_element_type=jnp.float32)


def inverse_factor(panels):
    vectors = len(panels) * SUB
    lane = lax.broadcasted_iota(jnp.int32, (SUB, 2 * vectors), 1)
    sub = lax.broadcasted_iota(jnp.int32, (SUB, 2 * vectors), 0)
    rows = []
    for p, panel in enumerate(panels):
        unit = jnp.where(lane == vectors + p * SUB + sub, 1.0, 0.0)
        rows.append(jnp.where(lane < vectors, panel, unit))

    def spread(panel, p):
        return [jnp.broadcast_to(panel[:, p * SUB + q : p * SUB + q + 1], panel.shape) for q in range(SUB)]

    def row(value, q):
        return jnp.broadcast_to(value[q : q + 1, :], value.shape)

    for p in range(len(panels)):
        cols = spread(rows[p], p)
        pivots, heads, inverses = [], [], []
        scale = jnp.ones_like(rows[p])
        for q in range(SUB):
            head = row(rows[p], q)
            tops = [None if t < q else row(cols[t], q) for t in range(SUB)]
            inverse = 1.0 / tops[q]
            pivots.append(head)
            heads.append(tops)
            inverses.append(inverse)
            scale = jnp.where(sub == q, tops[q], scale)
            factor = jnp.where(sub > q, cols[q] * inverse, 0.0)
            rows[p] = rows[p] - factor * head
            for t in range(q + 1, SUB):
                cols[t] = cols[t] - factor * tops[t]
        for r in range(p + 1, len(panels)):
            cols = spread(rows[r], p)
            for q in range(SUB):
                factor = cols[q] * inverses[q]
                rows[r] = rows[r] - factor * pivots[q]
                for t in range(q + 1, SUB):
                    cols[t] = cols[t] - factor * heads[q][t]
        rows[p] = rows[p] * lax.rsqrt(scale)
    return jnp.concatenate(rows, axis=0)[:, vectors:]


def padded(gram):
    return jnp.concatenate([gram, jnp.zeros_like(gram)], axis=1)


def read_block(ref, block, vectors, per_chunk):
    part = math.gcd(vectors, per_chunk)
    pieces = []
    for row in range(block * vectors, (block + 1) * vectors, part):
        at = row % per_chunk
        pieces.append(ref[row // per_chunk, at : at + part, :])
    return pieces[0] if len(pieces) == 1 else jnp.concatenate(pieces, axis=0)


def write_block(ref, block, value, per_chunk):
    vectors = value.shape[0]
    part = math.gcd(vectors, per_chunk)
    for begin in range(0, vectors, part):
        row = block * vectors + begin
        at = row % per_chunk
        ref[row // per_chunk, at : at + part, :] = value[begin : begin + part]


def gram_panels(ref, per_chunk, vectors, count):
    return [ref[c, per_chunk : per_chunk + SUB, :] * (1.0 / count) for c in range(vectors // SUB)]


def scale_of(degree):
    return lax.rsqrt(degree.astype(jnp.float32))


def phase(data, degree, tiles, src, dst, used, blocks_out, out_chunks, forward, gram_count, send_gram, keep_raw):
    slots, tile, _ = tiles.shape
    blocks = degree.shape[0]
    begins = data.ndim == 2
    vectors = data.shape[0] if begins else tile // 2
    per_chunk = None if begins else blocks * vectors // data.shape[0]
    have_gram = gram_count is not None
    terms = 1 if begins else 2
    out_per = blocks_out * vectors // out_chunks
    out_rows = out_per + (SUB if send_gram else 0)
    steps = slots // GROUP
    dims = (((1,), (1,)), ((), ())) if forward else (((1,), (0,)), ((), ()))

    def body(src_ref, dst_ref, used_ref, data_ref, degree_ref, tiles_ref, out_ref, *rest):
        if keep_raw:
            raw_ref, x_ref, sums_ref, gram_ref = rest
        else:
            x_ref, sums_ref, gram_ref = rest
        step = pl.program_id(0)

        @pl.when(step == 0)
        def _():
            sums_ref[...] = jnp.zeros_like(sums_ref)
            if have_gram:
                inverse = inverse_factor(gram_panels(data_ref, per_chunk, vectors, gram_count))
            gram = jnp.zeros((vectors, vectors), jnp.float32)
            for first in range(0, blocks, WIDTH):
                group = range(first, first + WIDTH)
                weight = jnp.concatenate([scale_of(degree_ref[block]) for block in group], axis=1)
                if begins:
                    raw = data_ref[:, first * tile : (first + WIDTH) * tile]
                else:
                    raw = jnp.concatenate([read_block(data_ref, block, vectors, per_chunk) for block in group], axis=1)
                    if have_gram:
                        raw = dot(inverse, raw)
                    raw = raw * weight
                if send_gram:
                    gram = gram + dot(raw, raw, last=True)
                source = raw * weight
                high = source.astype(jnp.bfloat16)
                if terms == 2:
                    low = (source - high.astype(jnp.float32)).astype(jnp.bfloat16)
                for at, block in enumerate(group):
                    lanes = slice(at * tile, (at + 1) * tile)
                    x_ref[block, :vectors, :] = high[:, lanes]
                    if terms == 2:
                        x_ref[block, vectors:, :] = low[:, lanes]
                    if keep_raw:
                        raw_ref[block] = raw[:, lanes]
            if send_gram:
                gram_ref[...] = padded(gram)

        for slot in range(GROUP):
            at = step * GROUP + slot
            product = lax.dot_general(
                x_ref[src_ref[at]], tiles_ref[slot], dims, preferred_element_type=jnp.float32
            )
            if terms == 2:
                product = product[:vectors] + product[vectors:]
            sums_ref[jnp.where(at < used_ref[0], dst_ref[at], blocks_out)] += product

        @pl.when(step == steps - 1)
        def _():
            for block in range(blocks_out):
                write_block(out_ref, block, sums_ref[block], out_per)
            if send_gram:
                for c in range(out_chunks):
                    rows = gram_ref[c * SUB : (c + 1) * SUB, :] if c * SUB < vectors else jnp.zeros((SUB, tile), jnp.float32)
                    out_ref[c, out_per:, :] = rows

    out_shape = [jax.ShapeDtypeStruct((out_chunks, out_rows, tile), jnp.float32)]
    out_specs = [pl.BlockSpec((out_chunks, out_rows, tile), lambda i, *_: (0, 0, 0))]
    if keep_raw:
        out_shape.append(jax.ShapeDtypeStruct((blocks, vectors, tile), jnp.float32))
        out_specs.append(pl.BlockSpec((blocks, vectors, tile), lambda i, *_: (0, 0, 0)))
    return pl.pallas_call(
        body,
        grid_spec=pltpu.PrefetchScalarGridSpec(
            num_scalar_prefetch=3,
            grid=(steps,),
            in_specs=[
                pl.BlockSpec(data.shape, lambda i, *_: (0,) * data.ndim),
                pl.BlockSpec(degree.shape, lambda i, *_: (0, 0, 0)),
                pl.BlockSpec((GROUP, tile, tile), lambda i, *_: (i, 0, 0)),
            ],
            out_specs=out_specs,
            scratch_shapes=[
                pltpu.VMEM((blocks, terms * vectors, tile), jnp.bfloat16),
                pltpu.VMEM((blocks_out + 1, vectors, tile), jnp.float32),
                pltpu.VMEM((vectors, tile), jnp.float32),
            ],
        ),
        out_shape=out_shape,
        compiler_params=pltpu.CompilerParams(vmem_limit_bytes=PHASE_LIMIT),
        name="forward" if forward else "backward",
    )(src, dst, used, data, degree, tiles)


PHASE_LIMIT = 60 * 1024 * 1024
VMEM_LIMIT = 32 * 1024 * 1024


def call(body, inputs, shapes, name):
    return pl.pallas_call(
        body,
        in_specs=[VMEM] * len(inputs),
        out_specs=[VMEM] * len(shapes),
        out_shape=[jax.ShapeDtypeStruct(s, jnp.float32) for s in shapes],
        compiler_params=pltpu.CompilerParams(vmem_limit_bytes=VMEM_LIMIT),
        name=name,
    )(*inputs)


def total(ref, begin, end):
    value = ref[0, begin:end, :]
    for c in range(1, ref.shape[0]):
        value = value + ref[c, begin:end, :]
    return value


def exchange(data, axis):
    return lax.all_to_all(data, axis, 0, 0)


def sum_copies(got, copies):
    def body(got_ref, out_ref):
        mine = total(got_ref, 0, got_ref.shape[1])
        for c in range(copies):
            out_ref[c] = mine

    return call(body, [got], [(copies,) + got.shape[1:]], "sum_copies")[0]


def narrow_sum(chunks):
    return exchange(sum_copies(exchange(chunks, "narrow"), chunks.shape[0]), "narrow")


def wide_sum(chunks):
    near = ("y", "z_low")
    part = sum_copies(exchange(chunks, near), lax.axis_size("z_high"))
    return exchange(sum_copies(exchange(part, "z_high"), chunks.shape[0]), near)


def finish_items(data, degree, user_count, copies):
    chunks, _, tile = data.shape
    blocks = degree.shape[0]
    vectors = tile // 2
    per_chunk = blocks * vectors // chunks

    def body(data_ref, degree_ref, raw_ref, gram_ref, inverse_ref):
        inverse = inverse_factor(gram_panels(data_ref, per_chunk, vectors, user_count))
        inverse_ref[...] = inverse
        gram = jnp.zeros((vectors, vectors), jnp.float32)
        for first in range(0, blocks, WIDTH):
            group = range(first, first + WIDTH)
            weight = jnp.concatenate([scale_of(degree_ref[block]) for block in group], axis=1)
            raw = jnp.concatenate([read_block(data_ref, block, vectors, per_chunk) for block in group], axis=1)
            raw = dot(inverse, raw) * weight
            gram = gram + dot(raw, raw, last=True)
            raw_ref[:, first * tile : (first + WIDTH) * tile] = raw
        packed = jnp.concatenate([gram[: vectors // 2], gram[vectors // 2 :]], axis=1)
        for c in range(copies):
            gram_ref[c] = packed

    shapes = [(vectors, blocks * tile), (copies, vectors // 2, tile), (vectors, vectors)]
    return call(body, [data, degree], shapes, "finish_items")


def finish_users(raw, inverse):
    blocks, vectors, tile = raw.shape

    def body(raw_ref, inverse_ref, out_ref):
        for block in range(blocks):
            out_ref[:, block * tile : (block + 1) * tile] = dot(inverse_ref[...], raw_ref[block])

    return call(body, [raw, inverse], [(vectors, blocks * tile)], "finish_users")[0]


def finish_vectors(raw, grams, item_count):
    vectors, rows = raw.shape
    width = WIDTH * grams.shape[2]

    def body(raw_ref, grams_ref, out_ref):
        gram = total(grams_ref, 0, vectors // 2) * (1.0 / item_count)
        gram = jnp.concatenate([gram[:, :vectors], gram[:, vectors:]], axis=0)
        gram = padded(gram)
        inverse = inverse_factor([gram[at : at + SUB] for at in range(0, vectors, SUB)])
        for begin in range(0, rows, width):
            out_ref[:, begin : begin + width] = dot(inverse, raw_ref[:, begin : begin + width])

    return call(body, [raw, grams], [raw.shape], "finish_vectors")[0]


def local(tile_values, tile_row, tile_col, tile_count, user_degree, item_degree, start_vectors):
    vectors, item_rows = start_vectors.shape
    slot_count, tile, _ = tile_values.shape
    user_rows = user_degree.shape[0]
    user_blocks = user_rows // tile
    item_blocks = item_rows // tile
    narrow_count = lax.axis_size("narrow")
    near_count = lax.axis_size("y") * lax.axis_size("z_low")
    all_users = user_rows * near_count * lax.axis_size("z_high")
    all_items = item_rows * narrow_count
    users = user_degree.reshape(user_blocks, 1, tile)
    items = item_degree.reshape(item_blocks, 1, tile)

    item_data = start_vectors
    for step in range(ITERS):
        first, last = step == 0, step == ITERS - 1
        (terms,) = phase(
            item_data, items, tile_values, tile_col, tile_row, tile_count, user_blocks, narrow_count, True,
            None if first else all_users, not first, False,
        )
        user_data = narrow_sum(terms)
        out = phase(
            user_data, users, tile_values, tile_row, tile_col, tile_count, item_blocks, near_count, False,
            None if first else all_items, True, last,
        )
        item_data = wide_sum(out[0])
    user_raw = out[1]
    item_raw, grams, user_inverse = finish_items(item_data, items, all_users, narrow_count)
    grams = exchange(grams, "narrow")
    user_vectors = finish_users(user_raw, user_inverse)
    item_vectors = finish_vectors(item_raw, grams, all_items)
    return (user_vectors, item_vectors)


def solution(mesh):
    wide_count, narrow_count = mesh.devices.shape
    grid = mesh.devices.reshape(Y_CHIPS, wide_count // (Y_CHIPS * Z_PAIR), Z_PAIR, narrow_count)
    wide = ("y", "z_high", "z_low")
    owner = wide + ("narrow",)
    return jax.shard_map(
        local,
        mesh=Mesh(grid, owner),
        in_specs=(
            P(owner, None, None),
            P(owner),
            P(owner),
            P(owner),
            P(wide),
            P("narrow"),
            P(None, "narrow"),
        ),
        out_specs=(P(None, wide), P(None, "narrow")),
        check_vma=False,
    )
```

```python
import math

import jax
import jax.numpy as jnp
from jax import lax
from jax.experimental import pallas as pl
from jax.experimental.pallas import tpu as pltpu
from jax.sharding import Mesh, PartitionSpec as P

ITERS = 2
GROUP = 16
Y_CHIPS = 8
Z_PAIR = 2
SUB = 8
WIDTH = 4
VMEM_LIMIT = 16 * 1024 * 1024
FULL = lax.Precision.HIGHEST
VMEM = pl.BlockSpec(memory_space=pltpu.VMEM)
SMEM = pl.BlockSpec(memory_space=pltpu.SMEM)


def dot(a, b, last=False):
    dims = (((1,), (1,)), ((), ())) if last else (((1,), (0,)), ((), ()))
    return lax.dot_general(a, b, dims, precision=FULL, preferred_element_type=jnp.float32)


def inverse_factor(panels):
    vectors = len(panels) * SUB
    lane = lax.broadcasted_iota(jnp.int32, (SUB, 2 * vectors), 1)
    sub = lax.broadcasted_iota(jnp.int32, (SUB, 2 * vectors), 0)
    rows = []
    for p, panel in enumerate(panels):
        unit = jnp.where(lane == vectors + p * SUB + sub, 1.0, 0.0)
        rows.append(jnp.where(lane < vectors, panel, unit))

    def spread(panel, p):
        return [jnp.broadcast_to(panel[:, p * SUB + q : p * SUB + q + 1], panel.shape) for q in range(SUB)]

    def row(value, q):
        return jnp.broadcast_to(value[q : q + 1, :], value.shape)

    for p in range(len(panels)):
        cols = spread(rows[p], p)
        pivots, heads, inverses = [], [], []
        scale = jnp.ones_like(rows[p])
        for q in range(SUB):
            head = row(rows[p], q)
            tops = [None if t < q else row(cols[t], q) for t in range(SUB)]
            inverse = 1.0 / tops[q]
            pivots.append(head)
            heads.append(tops)
            inverses.append(inverse)
            scale = jnp.where(sub == q, tops[q], scale)
            factor = jnp.where(sub > q, cols[q] * inverse, 0.0)
            rows[p] = rows[p] - factor * head
            for t in range(q + 1, SUB):
                cols[t] = cols[t] - factor * tops[t]
        for r in range(p + 1, len(panels)):
            cols = spread(rows[r], p)
            for q in range(SUB):
                factor = cols[q] * inverses[q]
                rows[r] = rows[r] - factor * pivots[q]
                for t in range(q + 1, SUB):
                    cols[t] = cols[t] - factor * heads[q][t]
        rows[p] = rows[p] * lax.rsqrt(scale)
    return jnp.concatenate(rows, axis=0)[:, vectors:]


def padded(gram):
    return jnp.concatenate([gram, jnp.zeros_like(gram)], axis=1)


def read_block(ref, block, vectors, per_chunk):
    part = math.gcd(vectors, per_chunk)
    pieces = []
    for row in range(block * vectors, (block + 1) * vectors, part):
        at = row % per_chunk
        pieces.append(ref[row // per_chunk, at : at + part, :])
    return pieces[0] if len(pieces) == 1 else jnp.concatenate(pieces, axis=0)


def write_block(ref, block, value, per_chunk):
    vectors = value.shape[0]
    part = math.gcd(vectors, per_chunk)
    for begin in range(0, vectors, part):
        row = block * vectors + begin
        at = row % per_chunk
        ref[row // per_chunk, at : at + part, :] = value[begin : begin + part]


def gram_panels(ref, per_chunk, vectors, count):
    return [ref[c, per_chunk : per_chunk + SUB, :] * (1.0 / count) for c in range(vectors // SUB)]


def scale_of(degree):
    return lax.rsqrt(degree.astype(jnp.float32))


def phase(data, degree, tiles, src, dst, used, blocks_out, out_chunks, forward, gram_count, send_gram, keep_raw):
    slots, tile, _ = tiles.shape
    blocks = degree.shape[0]
    begins = data.ndim == 2
    vectors = data.shape[0] if begins else tile // 2
    per_chunk = None if begins else blocks * vectors // data.shape[0]
    have_gram = gram_count is not None
    terms = 1 if begins else 2
    out_per = blocks_out * vectors // out_chunks
    out_rows = out_per + (SUB if send_gram else 0)
    dims = (((1,), (1,)), ((), ())) if forward else (((1,), (0,)), ((), ()))

    def body(src_ref, dst_ref, used_ref, data_ref, degree_ref, tiles_ref, out_ref, *rest):
        if keep_raw:
            raw_ref, x_ref, sums_ref = rest
        else:
            x_ref, sums_ref = rest
        sums_ref[...] = jnp.zeros_like(sums_ref)
        if have_gram:
            inverse = inverse_factor(gram_panels(data_ref, per_chunk, vectors, gram_count))
        gram = jnp.zeros((vectors, vectors), jnp.float32)
        for first in range(0, blocks, WIDTH):
            group = range(first, first + WIDTH)
            weight = jnp.concatenate([scale_of(degree_ref[block]) for block in group], axis=1)
            if begins:
                raw = data_ref[:, first * tile : (first + WIDTH) * tile]
            else:
                raw = jnp.concatenate([read_block(data_ref, block, vectors, per_chunk) for block in group], axis=1)
                if have_gram:
                    raw = dot(inverse, raw)
                raw = raw * weight
            if send_gram:
                gram = gram + dot(raw, raw, last=True)
            source = raw * weight
            high = source.astype(jnp.bfloat16)
            if terms == 2:
                low = (source - high.astype(jnp.float32)).astype(jnp.bfloat16)
            for at, block in enumerate(group):
                lanes = slice(at * tile, (at + 1) * tile)
                x_ref[block, :vectors, :] = high[:, lanes]
                if terms == 2:
                    x_ref[block, vectors:, :] = low[:, lanes]
                if keep_raw:
                    raw_ref[block] = raw[:, lanes]
        if send_gram:
            both = padded(gram)
            for c in range(out_chunks):
                inside = c * SUB < vectors
                out_ref[c, out_per:, :] = both[c * SUB : (c + 1) * SUB] if inside else jnp.zeros((SUB, tile), jnp.float32)

        @pl.loop(0, slots // GROUP)
        def _(step):
            for slot in range(GROUP):
                at = step * GROUP + slot
                product = lax.dot_general(
                    x_ref[src_ref[at]], tiles_ref[at], dims, preferred_element_type=jnp.float32
                )
                if terms == 2:
                    product = product[:vectors] + product[vectors:]
                sums_ref[jnp.where(at < used_ref[0], dst_ref[at], blocks_out)] += product

        for block in range(blocks_out):
            write_block(out_ref, block, sums_ref[block], out_per)

    out_shape = [jax.ShapeDtypeStruct((out_chunks, out_rows, tile), jnp.float32)]
    if keep_raw:
        out_shape.append(jax.ShapeDtypeStruct((blocks, vectors, tile), jnp.float32))
    return pl.pallas_call(
        body,
        in_specs=[SMEM] * 3 + [VMEM] * 3,
        out_specs=[VMEM] * len(out_shape),
        scratch_shapes=[
            pltpu.VMEM((blocks, terms * vectors, tile), jnp.bfloat16),
            pltpu.VMEM((blocks_out + 1, vectors, tile), jnp.float32),
        ],
        out_shape=out_shape,
        compiler_params=pltpu.CompilerParams(vmem_limit_bytes=VMEM_LIMIT),
        name="forward" if forward else "backward",
    )(src, dst, used, data, degree, tiles)


def call(body, inputs, shapes, name):
    return pl.pallas_call(
        body,
        in_specs=[VMEM] * len(inputs),
        out_specs=[VMEM] * len(shapes),
        out_shape=[jax.ShapeDtypeStruct(s, jnp.float32) for s in shapes],
        compiler_params=pltpu.CompilerParams(vmem_limit_bytes=VMEM_LIMIT),
        name=name,
    )(*inputs)


def total(ref, begin, end):
    value = ref[0, begin:end, :]
    for c in range(1, ref.shape[0]):
        value = value + ref[c, begin:end, :]
    return value


def exchange(data, axis):
    return lax.all_to_all(data, axis, 0, 0)


def sum_copies(got, copies):
    def body(got_ref, out_ref):
        mine = total(got_ref, 0, got_ref.shape[1])
        for c in range(copies):
            out_ref[c] = mine

    return call(body, [got], [(copies,) + got.shape[1:]], "sum_copies")[0]


def narrow_sum(chunks):
    return exchange(sum_copies(exchange(chunks, "narrow"), chunks.shape[0]), "narrow")


def wide_sum(chunks):
    near = ("y", "z_low")
    part = sum_copies(exchange(chunks, near), lax.axis_size("z_high"))
    return exchange(sum_copies(exchange(part, "z_high"), chunks.shape[0]), near)


def finish_items(data, degree, user_count, copies):
    chunks, _, tile = data.shape
    blocks = degree.shape[0]
    vectors = tile // 2
    per_chunk = blocks * vectors // chunks

    def body(data_ref, degree_ref, raw_ref, gram_ref, inverse_ref):
        inverse = inverse_factor(gram_panels(data_ref, per_chunk, vectors, user_count))
        inverse_ref[...] = inverse
        gram = jnp.zeros((vectors, vectors), jnp.float32)
        for first in range(0, blocks, WIDTH):
            group = range(first, first + WIDTH)
            weight = jnp.concatenate([scale_of(degree_ref[block]) for block in group], axis=1)
            raw = jnp.concatenate([read_block(data_ref, block, vectors, per_chunk) for block in group], axis=1)
            raw = dot(inverse, raw) * weight
            gram = gram + dot(raw, raw, last=True)
            raw_ref[:, first * tile : (first + WIDTH) * tile] = raw
        packed = jnp.concatenate([gram[: vectors // 2], gram[vectors // 2 :]], axis=1)
        for c in range(copies):
            gram_ref[c] = packed

    shapes = [(vectors, blocks * tile), (copies, vectors // 2, tile), (vectors, vectors)]
    return call(body, [data, degree], shapes, "finish_items")


def finish_users(raw, inverse):
    blocks, vectors, tile = raw.shape

    def body(raw_ref, inverse_ref, out_ref):
        for block in range(blocks):
            out_ref[:, block * tile : (block + 1) * tile] = dot(inverse_ref[...], raw_ref[block])

    return call(body, [raw, inverse], [(vectors, blocks * tile)], "finish_users")[0]


def finish_vectors(raw, grams, item_count):
    vectors, rows = raw.shape
    width = WIDTH * grams.shape[2]

    def body(raw_ref, grams_ref, out_ref):
        gram = total(grams_ref, 0, vectors // 2) * (1.0 / item_count)
        gram = jnp.concatenate([gram[:, :vectors], gram[:, vectors:]], axis=0)
        gram = padded(gram)
        inverse = inverse_factor([gram[at : at + SUB] for at in range(0, vectors, SUB)])
        for begin in range(0, rows, width):
            out_ref[:, begin : begin + width] = dot(inverse, raw_ref[:, begin : begin + width])

    return call(body, [raw, grams], [raw.shape], "finish_vectors")[0]


def local(tile_values, tile_row, tile_col, tile_count, user_degree, item_degree, start_vectors):
    vectors, item_rows = start_vectors.shape
    slot_count, tile, _ = tile_values.shape
    user_rows = user_degree.shape[0]
    user_blocks = user_rows // tile
    item_blocks = item_rows // tile
    narrow_count = lax.axis_size("narrow")
    near_count = lax.axis_size("y") * lax.axis_size("z_low")
    all_users = user_rows * near_count * lax.axis_size("z_high")
    all_items = item_rows * narrow_count
    users = user_degree.reshape(user_blocks, 1, tile)
    items = item_degree.reshape(item_blocks, 1, tile)

    item_data = start_vectors
    for step in range(ITERS):
        first, last = step == 0, step == ITERS - 1
        (terms,) = phase(
            item_data, items, tile_values, tile_col, tile_row, tile_count, user_blocks, narrow_count, True,
            None if first else all_users, not first, False,
        )
        user_data = narrow_sum(terms)
        out = phase(
            user_data, users, tile_values, tile_row, tile_col, tile_count, item_blocks, near_count, False,
            None if first else all_items, True, last,
        )
        item_data = wide_sum(out[0])
    user_raw = out[1]
    item_raw, grams, user_inverse = finish_items(item_data, items, all_users, narrow_count)
    grams = exchange(grams, "narrow")
    user_vectors = finish_users(user_raw, user_inverse)
    item_vectors = finish_vectors(item_raw, grams, all_items)
    return (user_vectors, item_vectors)


def solution(mesh):
    wide_count, narrow_count = mesh.devices.shape
    grid = mesh.devices.reshape(Y_CHIPS, wide_count // (Y_CHIPS * Z_PAIR), Z_PAIR, narrow_count)
    wide = ("y", "z_high", "z_low")
    owner = wide + ("narrow",)
    return jax.shard_map(
        local,
        mesh=Mesh(grid, owner),
        in_specs=(
            P(owner, None, None),
            P(owner),
            P(owner),
            P(owner),
            P(wide),
            P("narrow"),
            P(None, "narrow"),
        ),
        out_specs=(P(None, wide), P(None, "narrow")),
        check_vma=False,
    )
```

```python
import math

import jax
import jax.numpy as jnp
from jax import lax
from jax.experimental import pallas as pl
from jax.experimental.pallas import tpu as pltpu
from jax.sharding import Mesh, PartitionSpec as P

ITERS = 2
GROUP = 16
Y_CHIPS = 8
Z_PAIR = 2
SUB = 8
WIDTH = 4
VMEM_LIMIT = 16 * 1024 * 1024
BEGIN_LIMIT = 57 * 1024 * 1024
FULL = lax.Precision.HIGHEST
VMEM = pl.BlockSpec(memory_space=pltpu.VMEM)
SMEM = pl.BlockSpec(memory_space=pltpu.SMEM)


def dot(a, b, last=False):
    dims = (((1,), (1,)), ((), ())) if last else (((1,), (0,)), ((), ()))
    return lax.dot_general(a, b, dims, precision=FULL, preferred_element_type=jnp.float32)


def inverse_factor(panels):
    vectors = len(panels) * SUB
    lane = lax.broadcasted_iota(jnp.int32, (SUB, 2 * vectors), 1)
    sub = lax.broadcasted_iota(jnp.int32, (SUB, 2 * vectors), 0)
    rows = []
    for p, panel in enumerate(panels):
        unit = jnp.where(lane == vectors + p * SUB + sub, 1.0, 0.0)
        rows.append(jnp.where(lane < vectors, panel, unit))

    def spread(panel, p):
        return [jnp.broadcast_to(panel[:, p * SUB + q : p * SUB + q + 1], panel.shape) for q in range(SUB)]

    def row(value, q):
        return jnp.broadcast_to(value[q : q + 1, :], value.shape)

    for p in range(len(panels)):
        cols = spread(rows[p], p)
        pivots, heads, inverses = [], [], []
        scale = jnp.ones_like(rows[p])
        for q in range(SUB):
            head = row(rows[p], q)
            tops = [None if t < q else row(cols[t], q) for t in range(SUB)]
            inverse = 1.0 / tops[q]
            pivots.append(head)
            heads.append(tops)
            inverses.append(inverse)
            scale = jnp.where(sub == q, tops[q], scale)
            factor = jnp.where(sub > q, cols[q] * inverse, 0.0)
            rows[p] = rows[p] - factor * head
            for t in range(q + 1, SUB):
                cols[t] = cols[t] - factor * tops[t]
        for r in range(p + 1, len(panels)):
            cols = spread(rows[r], p)
            for q in range(SUB):
                factor = cols[q] * inverses[q]
                rows[r] = rows[r] - factor * pivots[q]
                for t in range(q + 1, SUB):
                    cols[t] = cols[t] - factor * heads[q][t]
        rows[p] = rows[p] * lax.rsqrt(scale)
    return jnp.concatenate(rows, axis=0)[:, vectors:]


def padded(gram):
    return jnp.concatenate([gram, jnp.zeros_like(gram)], axis=1)


def read_block(ref, block, vectors, per_chunk):
    part = math.gcd(vectors, per_chunk)
    pieces = []
    for row in range(block * vectors, (block + 1) * vectors, part):
        at = row % per_chunk
        pieces.append(ref[row // per_chunk, at : at + part, :])
    return pieces[0] if len(pieces) == 1 else jnp.concatenate(pieces, axis=0)


def write_block(ref, block, value, per_chunk):
    vectors = value.shape[0]
    part = math.gcd(vectors, per_chunk)
    for begin in range(0, vectors, part):
        row = block * vectors + begin
        at = row % per_chunk
        ref[row // per_chunk, at : at + part, :] = value[begin : begin + part]


def gram_panels(ref, per_chunk, vectors, count):
    return [ref[c, per_chunk : per_chunk + SUB, :] * (1.0 / count) for c in range(vectors // SUB)]


def scale_of(degree):
    return lax.rsqrt(degree.astype(jnp.float32))


def phase(data, degree, tiles, src, dst, used, blocks_out, out_chunks, forward, gram_count, send_gram, keep_raw):
    slots, tile, _ = tiles.shape
    blocks = degree.shape[0]
    begins = data.ndim == 2
    vectors = data.shape[0] if begins else tile // 2
    per_chunk = None if begins else blocks * vectors // data.shape[0]
    have_gram = gram_count is not None
    terms = 1 if begins else 2
    out_per = blocks_out * vectors // out_chunks
    out_rows = out_per + (SUB if send_gram else 0)
    dims = (((1,), (1,)), ((), ())) if forward else (((1,), (0,)), ((), ()))

    def body(src_ref, dst_ref, used_ref, data_ref, degree_ref, tiles_ref, out_ref, *rest):
        if begins:
            x_ref, sums_ref, data_here, degree_here, tiles_here, whole_sem, group_sem = rest

            def group_copy(step):
                rows = pl.ds(step * GROUP, GROUP)
                return pltpu.make_async_copy(tiles_ref.at[rows], tiles_here.at[rows], group_sem.at[step])

            copies = [
                pltpu.make_async_copy(degree_ref, degree_here, whole_sem.at[0]),
                pltpu.make_async_copy(data_ref, data_here, whole_sem.at[1]),
            ]
            for copy in copies + [group_copy(step) for step in range(slots // GROUP)]:
                copy.start()
            for copy in copies:
                copy.wait()
            product_phase(src_ref, dst_ref, used_ref, data_here, degree_here, tiles_here, out_ref, None, x_ref, sums_ref, group_copy)
        elif keep_raw:
            raw_ref, x_ref, sums_ref = rest
            product_phase(src_ref, dst_ref, used_ref, data_ref, degree_ref, tiles_ref, out_ref, raw_ref, x_ref, sums_ref, None)
        else:
            x_ref, sums_ref = rest
            product_phase(src_ref, dst_ref, used_ref, data_ref, degree_ref, tiles_ref, out_ref, None, x_ref, sums_ref, None)

    def product_phase(src_ref, dst_ref, used_ref, data_ref, degree_ref, tiles_ref, out_ref, raw_ref, x_ref, sums_ref, copy_of):
        sums_ref[...] = jnp.zeros_like(sums_ref)
        if have_gram:
            inverse = inverse_factor(gram_panels(data_ref, per_chunk, vectors, gram_count))
        gram = jnp.zeros((vectors, vectors), jnp.float32)
        for first in range(0, blocks, WIDTH):
            group = range(first, first + WIDTH)
            weight = jnp.concatenate([scale_of(degree_ref[block]) for block in group], axis=1)
            if begins:
                raw = data_ref[:, first * tile : (first + WIDTH) * tile]
            else:
                raw = jnp.concatenate([read_block(data_ref, block, vectors, per_chunk) for block in group], axis=1)
                if have_gram:
                    raw = dot(inverse, raw)
                raw = raw * weight
            if send_gram:
                gram = gram + dot(raw, raw, last=True)
            source = raw * weight
            high = source.astype(jnp.bfloat16)
            if terms == 2:
                low = (source - high.astype(jnp.float32)).astype(jnp.bfloat16)
            for at, block in enumerate(group):
                lanes = slice(at * tile, (at + 1) * tile)
                x_ref[block, :vectors, :] = high[:, lanes]
                if terms == 2:
                    x_ref[block, vectors:, :] = low[:, lanes]
                if keep_raw:
                    raw_ref[block] = raw[:, lanes]
        if send_gram:
            both = padded(gram)
            for c in range(out_chunks):
                inside = c * SUB < vectors
                out_ref[c, out_per:, :] = both[c * SUB : (c + 1) * SUB] if inside else jnp.zeros((SUB, tile), jnp.float32)

        @pl.loop(0, slots // GROUP)
        def _(step):
            if copy_of is not None:
                copy_of(step).wait()
            for slot in range(GROUP):
                at = step * GROUP + slot
                product = lax.dot_general(
                    x_ref[src_ref[at]], tiles_ref[at], dims, preferred_element_type=jnp.float32
                )
                if terms == 2:
                    product = product[:vectors] + product[vectors:]
                sums_ref[jnp.where(at < used_ref[0], dst_ref[at], blocks_out)] += product

        for block in range(blocks_out):
            write_block(out_ref, block, sums_ref[block], out_per)

    out_shape = [jax.ShapeDtypeStruct((out_chunks, out_rows, tile), jnp.float32)]
    if keep_raw:
        out_shape.append(jax.ShapeDtypeStruct((blocks, vectors, tile), jnp.float32))
    scratch = [
        pltpu.VMEM((blocks, terms * vectors, tile), jnp.bfloat16),
        pltpu.VMEM((blocks_out + 1, vectors, tile), jnp.float32),
    ]
    if begins:
        scratch += [
            pltpu.VMEM(data.shape, data.dtype),
            pltpu.VMEM(degree.shape, degree.dtype),
            pltpu.VMEM(tiles.shape, tiles.dtype),
            pltpu.SemaphoreType.DMA((2,)),
            pltpu.SemaphoreType.DMA((slots // GROUP,)),
        ]
        return pl.pallas_call(
            body,
            grid_spec=pltpu.PrefetchScalarGridSpec(
                num_scalar_prefetch=3,
                grid=(1,),
                in_specs=[pl.BlockSpec(memory_space=pl.ANY)] * 3,
                out_specs=[VMEM],
                scratch_shapes=scratch,
            ),
            out_shape=out_shape,
            compiler_params=pltpu.CompilerParams(vmem_limit_bytes=BEGIN_LIMIT),
            name="forward_begin",
        )(src, dst, used, data, degree, tiles)
    return pl.pallas_call(
        body,
        in_specs=[SMEM] * 3 + [VMEM] * 3,
        out_specs=[VMEM] * len(out_shape),
        scratch_shapes=scratch,
        out_shape=out_shape,
        compiler_params=pltpu.CompilerParams(vmem_limit_bytes=VMEM_LIMIT),
        name="forward" if forward else "backward",
    )(src, dst, used, data, degree, tiles)


def call(body, inputs, shapes, name):
    return pl.pallas_call(
        body,
        in_specs=[VMEM] * len(inputs),
        out_specs=[VMEM] * len(shapes),
        out_shape=[jax.ShapeDtypeStruct(s, jnp.float32) for s in shapes],
        compiler_params=pltpu.CompilerParams(vmem_limit_bytes=VMEM_LIMIT),
        name=name,
    )(*inputs)


def total(ref, begin, end):
    value = ref[0, begin:end, :]
    for c in range(1, ref.shape[0]):
        value = value + ref[c, begin:end, :]
    return value


def exchange(data, axis):
    return lax.all_to_all(data, axis, 0, 0)


def sum_copies(got, copies):
    def body(got_ref, out_ref):
        mine = total(got_ref, 0, got_ref.shape[1])
        for c in range(copies):
            out_ref[c] = mine

    return call(body, [got], [(copies,) + got.shape[1:]], "sum_copies")[0]


def narrow_sum(chunks):
    return exchange(sum_copies(exchange(chunks, "narrow"), chunks.shape[0]), "narrow")


def wide_sum(chunks):
    near = ("y", "z_low")
    part = sum_copies(exchange(chunks, near), lax.axis_size("z_high"))
    return exchange(sum_copies(exchange(part, "z_high"), chunks.shape[0]), near)


def finish_items(data, degree, user_count, copies):
    chunks, _, tile = data.shape
    blocks = degree.shape[0]
    vectors = tile // 2
    per_chunk = blocks * vectors // chunks

    def body(data_ref, degree_ref, raw_ref, gram_ref, inverse_ref):
        inverse = inverse_factor(gram_panels(data_ref, per_chunk, vectors, user_count))
        inverse_ref[...] = inverse
        gram = jnp.zeros((vectors, vectors), jnp.float32)
        for first in range(0, blocks, WIDTH):
            group = range(first, first + WIDTH)
            weight = jnp.concatenate([scale_of(degree_ref[block]) for block in group], axis=1)
            raw = jnp.concatenate([read_block(data_ref, block, vectors, per_chunk) for block in group], axis=1)
            raw = dot(inverse, raw) * weight
            gram = gram + dot(raw, raw, last=True)
            raw_ref[:, first * tile : (first + WIDTH) * tile] = raw
        packed = jnp.concatenate([gram[: vectors // 2], gram[vectors // 2 :]], axis=1)
        for c in range(copies):
            gram_ref[c] = packed

    shapes = [(vectors, blocks * tile), (copies, vectors // 2, tile), (vectors, vectors)]
    return call(body, [data, degree], shapes, "finish_items")


def finish_users(raw, inverse):
    blocks, vectors, tile = raw.shape

    def body(raw_ref, inverse_ref, out_ref):
        for block in range(blocks):
            out_ref[:, block * tile : (block + 1) * tile] = dot(inverse_ref[...], raw_ref[block])

    return call(body, [raw, inverse], [(vectors, blocks * tile)], "finish_users")[0]


def finish_vectors(raw, grams, item_count):
    vectors, rows = raw.shape
    width = WIDTH * grams.shape[2]

    def body(raw_ref, grams_ref, out_ref):
        gram = total(grams_ref, 0, vectors // 2) * (1.0 / item_count)
        gram = jnp.concatenate([gram[:, :vectors], gram[:, vectors:]], axis=0)
        gram = padded(gram)
        inverse = inverse_factor([gram[at : at + SUB] for at in range(0, vectors, SUB)])
        for begin in range(0, rows, width):
            out_ref[:, begin : begin + width] = dot(inverse, raw_ref[:, begin : begin + width])

    return call(body, [raw, grams], [raw.shape], "finish_vectors")[0]


def local(tile_values, tile_row, tile_col, tile_count, user_degree, item_degree, start_vectors):
    vectors, item_rows = start_vectors.shape
    slot_count, tile, _ = tile_values.shape
    user_rows = user_degree.shape[0]
    user_blocks = user_rows // tile
    item_blocks = item_rows // tile
    narrow_count = lax.axis_size("narrow")
    near_count = lax.axis_size("y") * lax.axis_size("z_low")
    all_users = user_rows * near_count * lax.axis_size("z_high")
    all_items = item_rows * narrow_count
    users = user_degree.reshape(user_blocks, 1, tile)
    items = item_degree.reshape(item_blocks, 1, tile)

    item_data = start_vectors
    for step in range(ITERS):
        first, last = step == 0, step == ITERS - 1
        (terms,) = phase(
            item_data, items, tile_values, tile_col, tile_row, tile_count, user_blocks, narrow_count, True,
            None if first else all_users, not first, False,
        )
        user_data = narrow_sum(terms)
        out = phase(
            user_data, users, tile_values, tile_row, tile_col, tile_count, item_blocks, near_count, False,
            None if first else all_items, True, last,
        )
        item_data = wide_sum(out[0])
    user_raw = out[1]
    item_raw, grams, user_inverse = finish_items(item_data, items, all_users, narrow_count)
    grams = exchange(grams, "narrow")
    user_vectors = finish_users(user_raw, user_inverse)
    item_vectors = finish_vectors(item_raw, grams, all_items)
    return (user_vectors, item_vectors)


def solution(mesh):
    wide_count, narrow_count = mesh.devices.shape
    grid = mesh.devices.reshape(Y_CHIPS, wide_count // (Y_CHIPS * Z_PAIR), Z_PAIR, narrow_count)
    wide = ("y", "z_high", "z_low")
    owner = wide + ("narrow",)
    return jax.shard_map(
        local,
        mesh=Mesh(grid, owner),
        in_specs=(
            P(owner, None, None),
            P(owner),
            P(owner),
            P(owner),
            P(wide),
            P("narrow"),
            P(None, "narrow"),
        ),
        out_specs=(P(None, wide), P(None, "narrow")),
        check_vma=False,
    )
```

```python
import math

import jax
import jax.numpy as jnp
from jax import lax
from jax.experimental import pallas as pl
from jax.experimental.pallas import tpu as pltpu
from jax.sharding import Mesh, PartitionSpec as P

ITERS = 2
GROUP = 64
BEGIN_GROUP = 32
Y_CHIPS = 8
Z_PAIR = 2
SUB = 8
WIDTH = 4
VMEM_LIMIT = 16 * 1024 * 1024
BEGIN_LIMIT = 57 * 1024 * 1024
FULL = lax.Precision.HIGHEST
VMEM = pl.BlockSpec(memory_space=pltpu.VMEM)
SMEM = pl.BlockSpec(memory_space=pltpu.SMEM)


def dot(a, b, last=False):
    dims = (((1,), (1,)), ((), ())) if last else (((1,), (0,)), ((), ()))
    return lax.dot_general(a, b, dims, precision=FULL, preferred_element_type=jnp.float32)


def inverse_factor(panels):
    vectors = len(panels) * SUB
    lane = lax.broadcasted_iota(jnp.int32, (SUB, 2 * vectors), 1)
    sub = lax.broadcasted_iota(jnp.int32, (SUB, 2 * vectors), 0)
    rows = []
    for p, panel in enumerate(panels):
        unit = jnp.where(lane == vectors + p * SUB + sub, 1.0, 0.0)
        rows.append(jnp.where(lane < vectors, panel, unit))

    def spread(panel, p):
        return [jnp.broadcast_to(panel[:, p * SUB + q : p * SUB + q + 1], panel.shape) for q in range(SUB)]

    def row(value, q):
        return jnp.broadcast_to(value[q : q + 1, :], value.shape)

    for p in range(len(panels)):
        cols = spread(rows[p], p)
        pivots, heads, inverses = [], [], []
        scale = jnp.ones_like(rows[p])
        for q in range(SUB):
            head = row(rows[p], q)
            tops = [None if t < q else row(cols[t], q) for t in range(SUB)]
            inverse = 1.0 / tops[q]
            pivots.append(head)
            heads.append(tops)
            inverses.append(inverse)
            scale = jnp.where(sub == q, tops[q], scale)
            factor = jnp.where(sub > q, cols[q] * inverse, 0.0)
            rows[p] = rows[p] - factor * head
            for t in range(q + 1, SUB):
                cols[t] = cols[t] - factor * tops[t]
        for r in range(p + 1, len(panels)):
            cols = spread(rows[r], p)
            for q in range(SUB):
                factor = cols[q] * inverses[q]
                rows[r] = rows[r] - factor * pivots[q]
                for t in range(q + 1, SUB):
                    cols[t] = cols[t] - factor * heads[q][t]
        rows[p] = rows[p] * lax.rsqrt(scale)
    return jnp.concatenate(rows, axis=0)[:, vectors:]


def padded(gram):
    return jnp.concatenate([gram, jnp.zeros_like(gram)], axis=1)


def read_block(ref, block, vectors, per_chunk):
    part = math.gcd(vectors, per_chunk)
    pieces = []
    for row in range(block * vectors, (block + 1) * vectors, part):
        at = row % per_chunk
        pieces.append(ref[row // per_chunk, at : at + part, :])
    return pieces[0] if len(pieces) == 1 else jnp.concatenate(pieces, axis=0)


def write_block(ref, block, value, per_chunk):
    vectors = value.shape[0]
    part = math.gcd(vectors, per_chunk)
    for begin in range(0, vectors, part):
        row = block * vectors + begin
        at = row % per_chunk
        ref[row // per_chunk, at : at + part, :] = value[begin : begin + part]


def gram_panels(ref, per_chunk, vectors, count):
    return [ref[c, per_chunk : per_chunk + SUB, :] * (1.0 / count) for c in range(vectors // SUB)]


def scale_of(degree):
    return lax.rsqrt(degree.astype(jnp.float32))


def phase(data, degree, tiles, src, dst, used, blocks_out, out_chunks, forward, gram_count, send_gram, keep_raw):
    slots, tile, _ = tiles.shape
    blocks = degree.shape[0]
    begins = data.ndim == 2
    vectors = data.shape[0] if begins else tile // 2
    per_chunk = None if begins else blocks * vectors // data.shape[0]
    have_gram = gram_count is not None
    terms = 1 if begins else 2
    out_per = blocks_out * vectors // out_chunks
    out_rows = out_per + (SUB if send_gram else 0)
    group_slots = BEGIN_GROUP if begins else GROUP
    dims = (((1,), (1,)), ((), ())) if forward else (((1,), (0,)), ((), ()))

    def body(src_ref, dst_ref, used_ref, data_ref, degree_ref, tiles_ref, out_ref, *rest):
        if begins:
            x_ref, sums_ref, data_here, degree_here, tiles_here, whole_sem, group_sem = rest

            def group_copy(step):
                rows = pl.ds(step * group_slots, group_slots)
                return pltpu.make_async_copy(tiles_ref.at[rows], tiles_here.at[rows], group_sem.at[step])

            copies = [
                pltpu.make_async_copy(degree_ref, degree_here, whole_sem.at[0]),
                pltpu.make_async_copy(data_ref, data_here, whole_sem.at[1]),
            ]
            for copy in copies + [group_copy(step) for step in range(slots // group_slots)]:
                copy.start()
            for copy in copies:
                copy.wait()
            product_phase(src_ref, dst_ref, used_ref, data_here, degree_here, tiles_here, out_ref, None, x_ref, sums_ref, group_copy)
        elif keep_raw:
            raw_ref, x_ref, sums_ref = rest
            product_phase(src_ref, dst_ref, used_ref, data_ref, degree_ref, tiles_ref, out_ref, raw_ref, x_ref, sums_ref, None)
        else:
            x_ref, sums_ref = rest
            product_phase(src_ref, dst_ref, used_ref, data_ref, degree_ref, tiles_ref, out_ref, None, x_ref, sums_ref, None)

    def product_phase(src_ref, dst_ref, used_ref, data_ref, degree_ref, tiles_ref, out_ref, raw_ref, x_ref, sums_ref, copy_of):
        sums_ref[...] = jnp.zeros_like(sums_ref)
        if have_gram:
            inverse = inverse_factor(gram_panels(data_ref, per_chunk, vectors, gram_count))
        gram = jnp.zeros((vectors, vectors), jnp.float32)
        for first in range(0, blocks, WIDTH):
            group = range(first, first + WIDTH)
            weight = jnp.concatenate([scale_of(degree_ref[block]) for block in group], axis=1)
            if begins:
                raw = data_ref[:, first * tile : (first + WIDTH) * tile]
            else:
                raw = jnp.concatenate([read_block(data_ref, block, vectors, per_chunk) for block in group], axis=1)
                if have_gram:
                    raw = dot(inverse, raw)
                raw = raw * weight
            if send_gram:
                gram = gram + dot(raw, raw, last=True)
            source = raw * weight
            high = source.astype(jnp.bfloat16)
            if terms == 2:
                low = (source - high.astype(jnp.float32)).astype(jnp.bfloat16)
            for at, block in enumerate(group):
                lanes = slice(at * tile, (at + 1) * tile)
                x_ref[block, :vectors, :] = high[:, lanes]
                if terms == 2:
                    x_ref[block, vectors:, :] = low[:, lanes]
                if keep_raw:
                    raw_ref[block] = raw[:, lanes]
        if send_gram:
            both = padded(gram)
            for c in range(out_chunks):
                inside = c * SUB < vectors
                out_ref[c, out_per:, :] = both[c * SUB : (c + 1) * SUB] if inside else jnp.zeros((SUB, tile), jnp.float32)

        @pl.loop(0, slots // group_slots)
        def _(step):
            if copy_of is not None:
                copy_of(step).wait()
            for slot in range(group_slots):
                at = step * group_slots + slot
                product = lax.dot_general(
                    x_ref[src_ref[at]], tiles_ref[at], dims, preferred_element_type=jnp.float32
                )
                if terms == 2:
                    product = product[:vectors] + product[vectors:]
                sums_ref[jnp.where(at < used_ref[0], dst_ref[at], blocks_out)] += product

        for block in range(blocks_out):
            write_block(out_ref, block, sums_ref[block], out_per)

    out_shape = [jax.ShapeDtypeStruct((out_chunks, out_rows, tile), jnp.float32)]
    if keep_raw:
        out_shape.append(jax.ShapeDtypeStruct((blocks, vectors, tile), jnp.float32))
    scratch = [
        pltpu.VMEM((blocks, terms * vectors, tile), jnp.bfloat16),
        pltpu.VMEM((blocks_out + 1, vectors, tile), jnp.float32),
    ]
    if begins:
        scratch += [
            pltpu.VMEM(data.shape, data.dtype),
            pltpu.VMEM(degree.shape, degree.dtype),
            pltpu.VMEM(tiles.shape, tiles.dtype),
            pltpu.SemaphoreType.DMA((2,)),
            pltpu.SemaphoreType.DMA((slots // group_slots,)),
        ]
        return pl.pallas_call(
            body,
            grid_spec=pltpu.PrefetchScalarGridSpec(
                num_scalar_prefetch=3,
                grid=(1,),
                in_specs=[pl.BlockSpec(memory_space=pl.ANY)] * 3,
                out_specs=[VMEM],
                scratch_shapes=scratch,
            ),
            out_shape=out_shape,
            compiler_params=pltpu.CompilerParams(vmem_limit_bytes=BEGIN_LIMIT),
            name="forward_begin",
        )(src, dst, used, data, degree, tiles)
    return pl.pallas_call(
        body,
        in_specs=[SMEM] * 3 + [VMEM] * 3,
        out_specs=[VMEM] * len(out_shape),
        scratch_shapes=scratch,
        out_shape=out_shape,
        compiler_params=pltpu.CompilerParams(vmem_limit_bytes=VMEM_LIMIT),
        name="forward" if forward else "backward",
    )(src, dst, used, data, degree, tiles)


def call(body, inputs, shapes, name):
    return pl.pallas_call(
        body,
        in_specs=[VMEM] * len(inputs),
        out_specs=[VMEM] * len(shapes),
        out_shape=[jax.ShapeDtypeStruct(s, jnp.float32) for s in shapes],
        compiler_params=pltpu.CompilerParams(vmem_limit_bytes=VMEM_LIMIT),
        name=name,
    )(*inputs)


def total(ref, begin, end):
    value = ref[0, begin:end, :]
    for c in range(1, ref.shape[0]):
        value = value + ref[c, begin:end, :]
    return value


def exchange(data, axis):
    return lax.all_to_all(data, axis, 0, 0)


def sum_copies(got, copies):
    def body(got_ref, out_ref):
        mine = total(got_ref, 0, got_ref.shape[1])
        for c in range(copies):
            out_ref[c] = mine

    return call(body, [got], [(copies,) + got.shape[1:]], "sum_copies")[0]


def narrow_sum(chunks):
    return exchange(sum_copies(exchange(chunks, "narrow"), chunks.shape[0]), "narrow")


def wide_sum(chunks):
    near = ("y", "z_low")
    part = sum_copies(exchange(chunks, near), lax.axis_size("z_high"))
    return exchange(sum_copies(exchange(part, "z_high"), chunks.shape[0]), near)


def finish_items(data, degree, user_count, copies):
    chunks, _, tile = data.shape
    blocks = degree.shape[0]
    vectors = tile // 2
    per_chunk = blocks * vectors // chunks

    def body(data_ref, degree_ref, raw_ref, gram_ref, inverse_ref):
        inverse = inverse_factor(gram_panels(data_ref, per_chunk, vectors, user_count))
        inverse_ref[...] = inverse
        gram = jnp.zeros((vectors, vectors), jnp.float32)
        for first in range(0, blocks, WIDTH):
            group = range(first, first + WIDTH)
            weight = jnp.concatenate([scale_of(degree_ref[block]) for block in group], axis=1)
            raw = jnp.concatenate([read_block(data_ref, block, vectors, per_chunk) for block in group], axis=1)
            raw = dot(inverse, raw) * weight
            gram = gram + dot(raw, raw, last=True)
            raw_ref[:, first * tile : (first + WIDTH) * tile] = raw
        packed = jnp.concatenate([gram[: vectors // 2], gram[vectors // 2 :]], axis=1)
        for c in range(copies):
            gram_ref[c] = packed

    shapes = [(vectors, blocks * tile), (copies, vectors // 2, tile), (vectors, vectors)]
    return call(body, [data, degree], shapes, "finish_items")


def finish_users(raw, inverse):
    blocks, vectors, tile = raw.shape

    def body(raw_ref, inverse_ref, out_ref):
        for block in range(blocks):
            out_ref[:, block * tile : (block + 1) * tile] = dot(inverse_ref[...], raw_ref[block])

    return call(body, [raw, inverse], [(vectors, blocks * tile)], "finish_users")[0]


def finish_vectors(raw, grams, item_count):
    vectors, rows = raw.shape
    width = WIDTH * grams.shape[2]

    def body(raw_ref, grams_ref, out_ref):
        gram = total(grams_ref, 0, vectors // 2) * (1.0 / item_count)
        gram = jnp.concatenate([gram[:, :vectors], gram[:, vectors:]], axis=0)
        gram = padded(gram)
        inverse = inverse_factor([gram[at : at + SUB] for at in range(0, vectors, SUB)])
        for begin in range(0, rows, width):
            out_ref[:, begin : begin + width] = dot(inverse, raw_ref[:, begin : begin + width])

    return call(body, [raw, grams], [raw.shape], "finish_vectors")[0]


def local(tile_values, tile_row, tile_col, tile_count, user_degree, item_degree, start_vectors):
    vectors, item_rows = start_vectors.shape
    slot_count, tile, _ = tile_values.shape
    user_rows = user_degree.shape[0]
    user_blocks = user_rows // tile
    item_blocks = item_rows // tile
    narrow_count = lax.axis_size("narrow")
    near_count = lax.axis_size("y") * lax.axis_size("z_low")
    all_users = user_rows * near_count * lax.axis_size("z_high")
    all_items = item_rows * narrow_count
    users = user_degree.reshape(user_blocks, 1, tile)
    items = item_degree.reshape(item_blocks, 1, tile)

    item_data = start_vectors
    for step in range(ITERS):
        first, last = step == 0, step == ITERS - 1
        (terms,) = phase(
            item_data, items, tile_values, tile_col, tile_row, tile_count, user_blocks, narrow_count, True,
            None if first else all_users, not first, False,
        )
        user_data = narrow_sum(terms)
        out = phase(
            user_data, users, tile_values, tile_row, tile_col, tile_count, item_blocks, near_count, False,
            None if first else all_items, True, last,
        )
        item_data = wide_sum(out[0])
    user_raw = out[1]
    item_raw, grams, user_inverse = finish_items(item_data, items, all_users, narrow_count)
    grams = exchange(grams, "narrow")
    user_vectors = finish_users(user_raw, user_inverse)
    item_vectors = finish_vectors(item_raw, grams, all_items)
    return (user_vectors, item_vectors)


def solution(mesh):
    wide_count, narrow_count = mesh.devices.shape
    grid = mesh.devices.reshape(Y_CHIPS, wide_count // (Y_CHIPS * Z_PAIR), Z_PAIR, narrow_count)
    wide = ("y", "z_high", "z_low")
    owner = wide + ("narrow",)
    return jax.shard_map(
        local,
        mesh=Mesh(grid, owner),
        in_specs=(
            P(owner, None, None),
            P(owner),
            P(owner),
            P(owner),
            P(wide),
            P("narrow"),
            P(None, "narrow"),
        ),
        out_specs=(P(None, wide), P(None, "narrow")),
        check_vma=False,
    )
```

```python
import math

import jax
import jax.numpy as jnp
from jax import lax
from jax.experimental import pallas as pl
from jax.experimental.pallas import tpu as pltpu
from jax.sharding import Mesh, PartitionSpec as P

ITERS = 2
GROUP = 64
BEGIN_GROUP = 32
Y_CHIPS = 8
Z_PAIR = 2
SUB = 8
WIDTH = 4
VMEM_LIMIT = 16 * 1024 * 1024
BEGIN_LIMIT = 57 * 1024 * 1024
FULL = lax.Precision.HIGHEST
VMEM = pl.BlockSpec(memory_space=pltpu.VMEM)
SMEM = pl.BlockSpec(memory_space=pltpu.SMEM)


def dot(a, b, last=False):
    dims = (((1,), (1,)), ((), ())) if last else (((1,), (0,)), ((), ()))
    return lax.dot_general(a, b, dims, precision=FULL, preferred_element_type=jnp.float32)


def inverse_factor(panels):
    vectors = len(panels) * SUB
    lane = lax.broadcasted_iota(jnp.int32, (SUB, 2 * vectors), 1)
    sub = lax.broadcasted_iota(jnp.int32, (SUB, 2 * vectors), 0)
    rows = []
    for p, panel in enumerate(panels):
        unit = jnp.where(lane == vectors + p * SUB + sub, 1.0, 0.0)
        rows.append(jnp.where(lane < vectors, panel, unit))

    def spread(panel, p):
        return [jnp.broadcast_to(panel[:, p * SUB + q : p * SUB + q + 1], panel.shape) for q in range(SUB)]

    def row(value, q):
        return jnp.broadcast_to(value[q : q + 1, :], value.shape)

    for p in range(len(panels)):
        cols = spread(rows[p], p)
        pivots, heads, inverses = [], [], []
        scale = jnp.ones_like(rows[p])
        for q in range(SUB):
            head = row(rows[p], q)
            tops = [None if t < q else row(cols[t], q) for t in range(SUB)]
            inverse = 1.0 / tops[q]
            pivots.append(head)
            heads.append(tops)
            inverses.append(inverse)
            scale = jnp.where(sub == q, tops[q], scale)
            factor = jnp.where(sub > q, cols[q] * inverse, 0.0)
            rows[p] = rows[p] - factor * head
            for t in range(q + 1, SUB):
                cols[t] = cols[t] - factor * tops[t]
        for r in range(p + 1, len(panels)):
            cols = spread(rows[r], p)
            for q in range(SUB):
                factor = cols[q] * inverses[q]
                rows[r] = rows[r] - factor * pivots[q]
                for t in range(q + 1, SUB):
                    cols[t] = cols[t] - factor * heads[q][t]
        rows[p] = rows[p] * lax.rsqrt(scale)
    return jnp.concatenate(rows, axis=0)[:, vectors:]


def read_block(ref, block, vectors, per_chunk, stride):
    part = math.gcd(vectors, per_chunk)
    pieces = []
    for row in range(block * vectors, (block + 1) * vectors, part):
        at = row // per_chunk * stride + row % per_chunk
        pieces.append(ref[at : at + part, :])
    return pieces[0] if len(pieces) == 1 else jnp.concatenate(pieces, axis=0)


def write_block(ref, block, value, per_chunk, stride):
    vectors = value.shape[0]
    part = math.gcd(vectors, per_chunk)
    for begin in range(0, vectors, part):
        row = block * vectors + begin
        at = row // per_chunk * stride + row % per_chunk
        ref[at : at + part, :] = value[begin : begin + part]


def pack(gram):
    half = gram.shape[0] // 2
    return jnp.concatenate([gram[:half], gram[half:]], axis=1)


def unpacked_panels(packed):
    vectors = packed.shape[1] // 2
    turned = jnp.concatenate([packed[:, vectors:], packed[:, :vectors]], axis=1)
    return [half[at : at + SUB] for half in (packed, turned) for at in range(0, vectors // 2, SUB)]


def gram_panels(ref, chunks, per_chunk, vectors, count):
    part = vectors // 2 // chunks
    stride = per_chunk + part
    rows = [ref[c * stride + per_chunk : (c + 1) * stride, :] for c in range(chunks)]
    return unpacked_panels(jnp.concatenate(rows, axis=0) * (1.0 / count))


def scale_of(degree):
    return lax.rsqrt(degree.astype(jnp.float32))


def phase(data, chunks, degree, tiles, src, dst, used, blocks_out, out_chunks, forward, gram_count, send_gram, keep_raw):
    slots, tile, _ = tiles.shape
    blocks = degree.shape[0]
    begins = chunks is None
    vectors = data.shape[0] if begins else tile // 2
    per_chunk = None if begins else blocks * vectors // chunks
    stride = None if begins else data.shape[0] // chunks
    have_gram = gram_count is not None
    terms = 1 if begins else 2
    out_per = blocks_out * vectors // out_chunks
    gram_rows = vectors // 2 // out_chunks if send_gram else 0
    out_stride = out_per + gram_rows
    group_slots = BEGIN_GROUP if begins else GROUP
    dims = (((1,), (1,)), ((), ())) if forward else (((1,), (0,)), ((), ()))

    def body(src_ref, dst_ref, used_ref, data_ref, degree_ref, tiles_ref, out_ref, *rest):
        if begins:
            x_ref, sums_ref, data_here, degree_here, tiles_here, whole_sem, group_sem = rest

            def group_copy(step):
                rows = pl.ds(step * group_slots, group_slots)
                return pltpu.make_async_copy(tiles_ref.at[rows], tiles_here.at[rows], group_sem.at[step])

            copies = [
                pltpu.make_async_copy(degree_ref, degree_here, whole_sem.at[0]),
                pltpu.make_async_copy(data_ref, data_here, whole_sem.at[1]),
            ]
            for copy in copies + [group_copy(step) for step in range(slots // group_slots)]:
                copy.start()
            for copy in copies:
                copy.wait()
            product_phase(src_ref, dst_ref, used_ref, data_here, degree_here, tiles_here, out_ref, None, x_ref, sums_ref, group_copy)
        elif keep_raw:
            raw_ref, x_ref, sums_ref = rest
            product_phase(src_ref, dst_ref, used_ref, data_ref, degree_ref, tiles_ref, out_ref, raw_ref, x_ref, sums_ref, None)
        else:
            x_ref, sums_ref = rest
            product_phase(src_ref, dst_ref, used_ref, data_ref, degree_ref, tiles_ref, out_ref, None, x_ref, sums_ref, None)

    def product_phase(src_ref, dst_ref, used_ref, data_ref, degree_ref, tiles_ref, out_ref, raw_ref, x_ref, sums_ref, copy_of):
        sums_ref[...] = jnp.zeros_like(sums_ref)
        if have_gram:
            inverse = inverse_factor(gram_panels(data_ref, chunks, per_chunk, vectors, gram_count))
        gram = jnp.zeros((vectors, vectors), jnp.float32)
        for first in range(0, blocks, WIDTH):
            group = range(first, first + WIDTH)
            weight = jnp.concatenate([scale_of(degree_ref[block]) for block in group], axis=1)
            if begins:
                raw = data_ref[:, first * tile : (first + WIDTH) * tile]
            else:
                raw = jnp.concatenate([read_block(data_ref, block, vectors, per_chunk, stride) for block in group], axis=1)
                if have_gram:
                    raw = dot(inverse, raw)
                raw = raw * weight
            if send_gram:
                gram = gram + dot(raw, raw, last=True)
            source = raw * weight
            high = source.astype(jnp.bfloat16)
            if terms == 2:
                low = (source - high.astype(jnp.float32)).astype(jnp.bfloat16)
            for at, block in enumerate(group):
                lanes = slice(at * tile, (at + 1) * tile)
                x_ref[block, :vectors, :] = high[:, lanes]
                if terms == 2:
                    x_ref[block, vectors:, :] = low[:, lanes]
                if keep_raw:
                    raw_ref[block] = raw[:, lanes]
        if send_gram:
            packed = pack(gram)
            for c in range(out_chunks):
                at = c * out_stride + out_per
                out_ref[at : at + gram_rows, :] = packed[c * gram_rows : (c + 1) * gram_rows]

        @pl.loop(0, slots // group_slots)
        def _(step):
            if copy_of is not None:
                copy_of(step).wait()
            for slot in range(group_slots):
                at = step * group_slots + slot
                product = lax.dot_general(
                    x_ref[src_ref[at]], tiles_ref[at], dims, preferred_element_type=jnp.float32
                )
                if terms == 2:
                    product = product[:vectors] + product[vectors:]
                sums_ref[jnp.where(at < used_ref[0], dst_ref[at], blocks_out)] += product

        for block in range(blocks_out):
            write_block(out_ref, block, sums_ref[block], out_per, out_stride)

    out_shape = [jax.ShapeDtypeStruct((out_chunks * out_stride, tile), jnp.float32)]
    if keep_raw:
        out_shape.append(jax.ShapeDtypeStruct((blocks, vectors, tile), jnp.float32))
    scratch = [
        pltpu.VMEM((blocks, terms * vectors, tile), jnp.bfloat16),
        pltpu.VMEM((blocks_out + 1, vectors, tile), jnp.float32),
    ]
    if begins:
        scratch += [
            pltpu.VMEM(data.shape, data.dtype),
            pltpu.VMEM(degree.shape, degree.dtype),
            pltpu.VMEM(tiles.shape, tiles.dtype),
            pltpu.SemaphoreType.DMA((2,)),
            pltpu.SemaphoreType.DMA((slots // group_slots,)),
        ]
        return pl.pallas_call(
            body,
            grid_spec=pltpu.PrefetchScalarGridSpec(
                num_scalar_prefetch=3,
                grid=(1,),
                in_specs=[pl.BlockSpec(memory_space=pl.ANY)] * 3,
                out_specs=[VMEM],
                scratch_shapes=scratch,
            ),
            out_shape=out_shape,
            compiler_params=pltpu.CompilerParams(vmem_limit_bytes=BEGIN_LIMIT),
            name="forward_begin",
        )(src, dst, used, data, degree, tiles)
    return pl.pallas_call(
        body,
        in_specs=[SMEM] * 3 + [VMEM] * 3,
        out_specs=[VMEM] * len(out_shape),
        scratch_shapes=scratch,
        out_shape=out_shape,
        compiler_params=pltpu.CompilerParams(vmem_limit_bytes=VMEM_LIMIT),
        name="forward" if forward else "backward",
    )(src, dst, used, data, degree, tiles)


def call(body, inputs, shapes, name):
    return pl.pallas_call(
        body,
        in_specs=[VMEM] * len(inputs),
        out_specs=[VMEM] * len(shapes),
        out_shape=[jax.ShapeDtypeStruct(s, jnp.float32) for s in shapes],
        compiler_params=pltpu.CompilerParams(vmem_limit_bytes=VMEM_LIMIT),
        name=name,
    )(*inputs)


def exchange(data, axis, count):
    return lax.all_to_all(data.reshape(count, 1, -1), axis, 0, 0).reshape(data.shape)


def sum_copies(got, count, copies, rows, stride):
    step = got.shape[0] // count

    def body(got_ref, out_ref):
        mine = got_ref[:rows, :]
        for c in range(1, count):
            mine = mine + got_ref[c * step : c * step + rows, :]
        if stride > rows:
            mine = jnp.concatenate([mine, jnp.zeros((stride - rows, mine.shape[1]), jnp.float32)], axis=0)
        for c in range(copies):
            out_ref[c * stride : (c + 1) * stride, :] = mine

    return call(body, [got], [(copies * stride, got.shape[1])], "sum_copies")[0]


def narrow_sum(data):
    count = lax.axis_size("narrow")
    rows = data.shape[0] // count
    return exchange(sum_copies(exchange(data, "narrow", count), count, count, rows, rows), "narrow", count)


def wide_sum(data):
    near = ("y", "z_low")
    near_count, far_count = lax.axis_size("y") * lax.axis_size("z_low"), lax.axis_size("z_high")
    rows = data.shape[0] // near_count
    stride = -(-rows // SUB) * SUB
    part = sum_copies(exchange(data, near, near_count), near_count, far_count, rows, stride)
    back = sum_copies(exchange(part, "z_high", far_count), far_count, near_count, rows, rows)
    return exchange(back, near, near_count)


def finish_items(data, chunks, degree, user_count, copies):
    rows, tile = data.shape
    blocks = degree.shape[0]
    vectors = tile // 2
    per_chunk = blocks * vectors // chunks
    stride = rows // chunks

    def body(data_ref, degree_ref, raw_ref, gram_ref, inverse_ref):
        inverse = inverse_factor(gram_panels(data_ref, chunks, per_chunk, vectors, user_count))
        inverse_ref[...] = inverse
        gram = jnp.zeros((vectors, vectors), jnp.float32)
        for first in range(0, blocks, WIDTH):
            group = range(first, first + WIDTH)
            weight = jnp.concatenate([scale_of(degree_ref[block]) for block in group], axis=1)
            raw = jnp.concatenate([read_block(data_ref, block, vectors, per_chunk, stride) for block in group], axis=1)
            raw = dot(inverse, raw) * weight
            gram = gram + dot(raw, raw, last=True)
            raw_ref[:, first * tile : (first + WIDTH) * tile] = raw
        packed = pack(gram)
        for c in range(copies):
            gram_ref[c * vectors // 2 : (c + 1) * vectors // 2, :] = packed

    shapes = [(vectors, blocks * tile), (copies * vectors // 2, tile), (vectors, vectors)]
    return call(body, [data, degree], shapes, "finish_items")


def finish_users(raw, inverse):
    blocks, vectors, tile = raw.shape

    def body(raw_ref, inverse_ref, out_ref):
        for block in range(blocks):
            out_ref[:, block * tile : (block + 1) * tile] = dot(inverse_ref[...], raw_ref[block])

    return call(body, [raw, inverse], [(vectors, blocks * tile)], "finish_users")[0]


def finish_vectors(raw, grams, item_count):
    vectors, rows = raw.shape
    half = vectors // 2
    width = WIDTH * grams.shape[1]

    def body(raw_ref, grams_ref, out_ref):
        packed = grams_ref[:half, :]
        for at in range(half, grams.shape[0], half):
            packed = packed + grams_ref[at : at + half, :]
        inverse = inverse_factor(unpacked_panels(packed * (1.0 / item_count)))
        for begin in range(0, rows, width):
            out_ref[:, begin : begin + width] = dot(inverse, raw_ref[:, begin : begin + width])

    return call(body, [raw, grams], [raw.shape], "finish_vectors")[0]


def local(tile_values, tile_row, tile_col, tile_count, user_degree, item_degree, start_vectors):
    vectors, item_rows = start_vectors.shape
    slot_count, tile, _ = tile_values.shape
    user_rows = user_degree.shape[0]
    user_blocks = user_rows // tile
    item_blocks = item_rows // tile
    narrow_count = lax.axis_size("narrow")
    near_count = lax.axis_size("y") * lax.axis_size("z_low")
    all_users = user_rows * near_count * lax.axis_size("z_high")
    all_items = item_rows * narrow_count
    users = user_degree.reshape(user_blocks, 1, tile)
    items = item_degree.reshape(item_blocks, 1, tile)

    item_data = start_vectors
    for step in range(ITERS):
        first, last = step == 0, step == ITERS - 1
        (terms,) = phase(
            item_data, None if first else near_count, items, tile_values, tile_col, tile_row, tile_count, user_blocks, narrow_count, True,
            None if first else all_users, not first, False,
        )
        user_data = narrow_sum(terms)
        out = phase(
            user_data, narrow_count, users, tile_values, tile_row, tile_col, tile_count, item_blocks, near_count, False,
            None if first else all_items, True, last,
        )
        item_data = wide_sum(out[0])
    user_raw = out[1]
    item_raw, grams, user_inverse = finish_items(item_data, near_count, items, all_users, narrow_count)
    grams = exchange(grams, "narrow", narrow_count)
    user_vectors = finish_users(user_raw, user_inverse)
    item_vectors = finish_vectors(item_raw, grams, all_items)
    return (user_vectors, item_vectors)


def solution(mesh):
    wide_count, narrow_count = mesh.devices.shape
    grid = mesh.devices.reshape(Y_CHIPS, wide_count // (Y_CHIPS * Z_PAIR), Z_PAIR, narrow_count)
    wide = ("y", "z_high", "z_low")
    owner = wide + ("narrow",)
    return jax.shard_map(
        local,
        mesh=Mesh(grid, owner),
        in_specs=(
            P(owner, None, None),
            P(owner),
            P(owner),
            P(owner),
            P(wide),
            P("narrow"),
            P(None, "narrow"),
        ),
        out_specs=(P(None, wide), P(None, "narrow")),
        check_vma=False,
    )
```

```python
import math

import jax
import jax.numpy as jnp
from jax import lax
from jax.experimental import pallas as pl
from jax.experimental.pallas import tpu as pltpu
from jax.sharding import Mesh, PartitionSpec as P

ITERS = 2
GROUP = 128
BEGIN_GROUP = 32
Y_CHIPS = 8
Z_PAIR = 2
SUB = 8
WIDTH = 4
VMEM_LIMIT = 16 * 1024 * 1024
BEGIN_LIMIT = 57 * 1024 * 1024
FULL = lax.Precision.HIGHEST
VMEM = pl.BlockSpec(memory_space=pltpu.VMEM)
SMEM = pl.BlockSpec(memory_space=pltpu.SMEM)


def dot(a, b, last=False):
    dims = (((1,), (1,)), ((), ())) if last else (((1,), (0,)), ((), ()))
    return lax.dot_general(a, b, dims, precision=FULL, preferred_element_type=jnp.float32)


def inverse_factor(panels):
    vectors = len(panels) * SUB
    lane = lax.broadcasted_iota(jnp.int32, (SUB, 2 * vectors), 1)
    sub = lax.broadcasted_iota(jnp.int32, (SUB, 2 * vectors), 0)
    rows = []
    for p, panel in enumerate(panels):
        unit = jnp.where(lane == vectors + p * SUB + sub, 1.0, 0.0)
        rows.append(jnp.where(lane < vectors, panel, unit))

    def spread(panel, p):
        return [jnp.broadcast_to(panel[:, p * SUB + q : p * SUB + q + 1], panel.shape) for q in range(SUB)]

    def row(value, q):
        return jnp.broadcast_to(value[q : q + 1, :], value.shape)

    for p in range(len(panels)):
        cols = spread(rows[p], p)
        pivots, heads, inverses = [], [], []
        scale = jnp.ones_like(rows[p])
        for q in range(SUB):
            head = row(rows[p], q)
            tops = [None if t < q else row(cols[t], q) for t in range(SUB)]
            inverse = 1.0 / tops[q]
            pivots.append(head)
            heads.append(tops)
            inverses.append(inverse)
            scale = jnp.where(sub == q, tops[q], scale)
            factor = jnp.where(sub > q, cols[q] * inverse, 0.0)
            rows[p] = rows[p] - factor * head
            for t in range(q + 1, SUB):
                cols[t] = cols[t] - factor * tops[t]
        for r in range(p + 1, len(panels)):
            cols = spread(rows[r], p)
            for q in range(SUB):
                factor = cols[q] * inverses[q]
                rows[r] = rows[r] - factor * pivots[q]
                for t in range(q + 1, SUB):
                    cols[t] = cols[t] - factor * heads[q][t]
        rows[p] = rows[p] * lax.rsqrt(scale)
    return jnp.concatenate(rows, axis=0)[:, vectors:]


def read_block(ref, block, vectors, per_chunk, stride):
    part = math.gcd(vectors, per_chunk)
    pieces = []
    for row in range(block * vectors, (block + 1) * vectors, part):
        at = row // per_chunk * stride + row % per_chunk
        pieces.append(ref[at : at + part, :])
    return pieces[0] if len(pieces) == 1 else jnp.concatenate(pieces, axis=0)


def write_block(ref, block, value, per_chunk, stride):
    vectors = value.shape[0]
    part = math.gcd(vectors, per_chunk)
    for begin in range(0, vectors, part):
        row = block * vectors + begin
        at = row // per_chunk * stride + row % per_chunk
        ref[at : at + part, :] = value[begin : begin + part]


def pack(gram):
    half = gram.shape[0] // 2
    return jnp.concatenate([gram[:half], gram[half:]], axis=1)


def unpacked_panels(packed):
    vectors = packed.shape[1] // 2
    turned = jnp.concatenate([packed[:, vectors:], packed[:, :vectors]], axis=1)
    return [half[at : at + SUB] for half in (packed, turned) for at in range(0, vectors // 2, SUB)]


def gram_panels(ref, chunks, per_chunk, vectors, count):
    part = vectors // 2 // chunks
    stride = per_chunk + part
    rows = [ref[c * stride + per_chunk : (c + 1) * stride, :] for c in range(chunks)]
    return unpacked_panels(jnp.concatenate(rows, axis=0) * (1.0 / count))


def scale_of(degree):
    return lax.rsqrt(degree.astype(jnp.float32))


def phase(data, chunks, degree, tiles, src, dst, used, blocks_out, out_chunks, forward, gram_count, send_gram, keep_raw):
    slots, tile, _ = tiles.shape
    blocks = degree.shape[0]
    begins = chunks is None
    vectors = data.shape[0] if begins else tile // 2
    per_chunk = None if begins else blocks * vectors // chunks
    stride = None if begins else data.shape[0] // chunks
    have_gram = gram_count is not None
    terms = 1 if begins else 2
    out_per = blocks_out * vectors // out_chunks
    gram_rows = vectors // 2 // out_chunks if send_gram else 0
    out_stride = out_per + gram_rows
    group_slots = BEGIN_GROUP if begins else GROUP
    dims = (((1,), (1,)), ((), ())) if forward else (((1,), (0,)), ((), ()))

    def body(src_ref, dst_ref, used_ref, data_ref, degree_ref, tiles_ref, out_ref, *rest):
        if begins:
            x_ref, sums_ref, data_here, degree_here, tiles_here, whole_sem, group_sem = rest

            def group_copy(step):
                rows = pl.ds(step * group_slots, group_slots)
                return pltpu.make_async_copy(tiles_ref.at[rows], tiles_here.at[rows], group_sem.at[step])

            copies = [
                pltpu.make_async_copy(degree_ref, degree_here, whole_sem.at[0]),
                pltpu.make_async_copy(data_ref, data_here, whole_sem.at[1]),
            ]
            for copy in copies + [group_copy(step) for step in range(slots // group_slots)]:
                copy.start()
            for copy in copies:
                copy.wait()
            product_phase(src_ref, dst_ref, used_ref, data_here, degree_here, tiles_here, out_ref, None, x_ref, sums_ref, group_copy)
        elif keep_raw:
            raw_ref, x_ref, sums_ref = rest
            product_phase(src_ref, dst_ref, used_ref, data_ref, degree_ref, tiles_ref, out_ref, raw_ref, x_ref, sums_ref, None)
        else:
            x_ref, sums_ref = rest
            product_phase(src_ref, dst_ref, used_ref, data_ref, degree_ref, tiles_ref, out_ref, None, x_ref, sums_ref, None)

    def product_phase(src_ref, dst_ref, used_ref, data_ref, degree_ref, tiles_ref, out_ref, raw_ref, x_ref, sums_ref, copy_of):
        sums_ref[...] = jnp.zeros_like(sums_ref)
        if have_gram:
            inverse = inverse_factor(gram_panels(data_ref, chunks, per_chunk, vectors, gram_count))
        gram = jnp.zeros((vectors, vectors), jnp.float32)
        for first in range(0, blocks, WIDTH):
            group = range(first, first + WIDTH)
            weight = jnp.concatenate([scale_of(degree_ref[block]) for block in group], axis=1)
            if begins:
                raw = data_ref[:, first * tile : (first + WIDTH) * tile]
            else:
                raw = jnp.concatenate([read_block(data_ref, block, vectors, per_chunk, stride) for block in group], axis=1)
                if have_gram:
                    raw = dot(inverse, raw)
                raw = raw * weight
            if send_gram:
                gram = gram + dot(raw, raw, last=True)
            source = raw * weight
            high = source.astype(jnp.bfloat16)
            if terms == 2:
                low = (source - high.astype(jnp.float32)).astype(jnp.bfloat16)
            for at, block in enumerate(group):
                lanes = slice(at * tile, (at + 1) * tile)
                x_ref[block, :vectors, :] = high[:, lanes]
                if terms == 2:
                    x_ref[block, vectors:, :] = low[:, lanes]
                if keep_raw:
                    raw_ref[block] = raw[:, lanes]
        if send_gram:
            packed = pack(gram)
            for c in range(out_chunks):
                at = c * out_stride + out_per
                out_ref[at : at + gram_rows, :] = packed[c * gram_rows : (c + 1) * gram_rows]

        @pl.loop(0, slots // group_slots)
        def _(step):
            if copy_of is not None:
                copy_of(step).wait()
            for slot in range(group_slots):
                at = step * group_slots + slot
                product = lax.dot_general(
                    x_ref[src_ref[at]], tiles_ref[at], dims, preferred_element_type=jnp.float32
                )
                if terms == 2:
                    product = product[:vectors] + product[vectors:]
                sums_ref[jnp.where(at < used_ref[0], dst_ref[at], blocks_out)] += product

        for block in range(blocks_out):
            write_block(out_ref, block, sums_ref[block], out_per, out_stride)

    out_shape = [jax.ShapeDtypeStruct((out_chunks * out_stride, tile), jnp.float32)]
    if keep_raw:
        out_shape.append(jax.ShapeDtypeStruct((blocks, vectors, tile), jnp.float32))
    scratch = [
        pltpu.VMEM((blocks, terms * vectors, tile), jnp.bfloat16),
        pltpu.VMEM((blocks_out + 1, vectors, tile), jnp.float32),
    ]
    if begins:
        scratch += [
            pltpu.VMEM(data.shape, data.dtype),
            pltpu.VMEM(degree.shape, degree.dtype),
            pltpu.VMEM(tiles.shape, tiles.dtype),
            pltpu.SemaphoreType.DMA((2,)),
            pltpu.SemaphoreType.DMA((slots // group_slots,)),
        ]
        return pl.pallas_call(
            body,
            grid_spec=pltpu.PrefetchScalarGridSpec(
                num_scalar_prefetch=3,
                grid=(1,),
                in_specs=[pl.BlockSpec(memory_space=pl.ANY)] * 3,
                out_specs=[VMEM],
                scratch_shapes=scratch,
            ),
            out_shape=out_shape,
            compiler_params=pltpu.CompilerParams(vmem_limit_bytes=BEGIN_LIMIT),
            name="forward_begin",
        )(src, dst, used, data, degree, tiles)
    return pl.pallas_call(
        body,
        in_specs=[SMEM] * 3 + [VMEM] * 3,
        out_specs=[VMEM] * len(out_shape),
        scratch_shapes=scratch,
        out_shape=out_shape,
        compiler_params=pltpu.CompilerParams(vmem_limit_bytes=VMEM_LIMIT),
        name="forward" if forward else "backward",
    )(src, dst, used, data, degree, tiles)


def call(body, inputs, shapes, name):
    return pl.pallas_call(
        body,
        in_specs=[VMEM] * len(inputs),
        out_specs=[VMEM] * len(shapes),
        out_shape=[jax.ShapeDtypeStruct(s, jnp.float32) for s in shapes],
        compiler_params=pltpu.CompilerParams(vmem_limit_bytes=VMEM_LIMIT),
        name=name,
    )(*inputs)


def exchange(data, axis, count):
    return lax.all_to_all(data.reshape(count, 1, -1), axis, 0, 0).reshape(data.shape)


def sum_copies(got, count, copies, rows, stride):
    step = got.shape[0] // count

    def body(got_ref, out_ref):
        mine = got_ref[:rows, :]
        for c in range(1, count):
            mine = mine + got_ref[c * step : c * step + rows, :]
        if stride > rows:
            mine = jnp.concatenate([mine, jnp.zeros((stride - rows, mine.shape[1]), jnp.float32)], axis=0)
        for c in range(copies):
            out_ref[c * stride : (c + 1) * stride, :] = mine

    return call(body, [got], [(copies * stride, got.shape[1])], "sum_copies")[0]


def narrow_sum(data):
    count = lax.axis_size("narrow")
    rows = data.shape[0] // count
    return exchange(sum_copies(exchange(data, "narrow", count), count, count, rows, rows), "narrow", count)


def wide_sum(data):
    near = ("y", "z_low")
    near_count, far_count = lax.axis_size("y") * lax.axis_size("z_low"), lax.axis_size("z_high")
    rows = data.shape[0] // near_count
    stride = -(-rows // SUB) * SUB
    part = sum_copies(exchange(data, near, near_count), near_count, far_count, rows, stride)
    back = sum_copies(exchange(part, "z_high", far_count), far_count, near_count, rows, rows)
    return exchange(back, near, near_count)


def finish_items(data, chunks, degree, user_count, copies):
    rows, tile = data.shape
    blocks = degree.shape[0]
    vectors = tile // 2
    per_chunk = blocks * vectors // chunks
    stride = rows // chunks

    def body(data_ref, degree_ref, raw_ref, gram_ref, inverse_ref):
        inverse = inverse_factor(gram_panels(data_ref, chunks, per_chunk, vectors, user_count))
        inverse_ref[...] = inverse
        gram = jnp.zeros((vectors, vectors), jnp.float32)
        for first in range(0, blocks, WIDTH):
            group = range(first, first + WIDTH)
            weight = jnp.concatenate([scale_of(degree_ref[block]) for block in group], axis=1)
            raw = jnp.concatenate([read_block(data_ref, block, vectors, per_chunk, stride) for block in group], axis=1)
            raw = dot(inverse, raw) * weight
            gram = gram + dot(raw, raw, last=True)
            raw_ref[:, first * tile : (first + WIDTH) * tile] = raw
        packed = pack(gram)
        for c in range(copies):
            gram_ref[c * vectors // 2 : (c + 1) * vectors // 2, :] = packed

    shapes = [(vectors, blocks * tile), (copies * vectors // 2, tile), (vectors, vectors)]
    return call(body, [data, degree], shapes, "finish_items")


def finish_users(raw, inverse):
    blocks, vectors, tile = raw.shape

    def body(raw_ref, inverse_ref, out_ref):
        for block in range(blocks):
            out_ref[:, block * tile : (block + 1) * tile] = dot(inverse_ref[...], raw_ref[block])

    return call(body, [raw, inverse], [(vectors, blocks * tile)], "finish_users")[0]


def finish_vectors(raw, grams, item_count):
    vectors, rows = raw.shape
    half = vectors // 2
    width = WIDTH * grams.shape[1]

    def body(raw_ref, grams_ref, out_ref):
        packed = grams_ref[:half, :]
        for at in range(half, grams.shape[0], half):
            packed = packed + grams_ref[at : at + half, :]
        inverse = inverse_factor(unpacked_panels(packed * (1.0 / item_count)))
        for begin in range(0, rows, width):
            out_ref[:, begin : begin + width] = dot(inverse, raw_ref[:, begin : begin + width])

    return call(body, [raw, grams], [raw.shape], "finish_vectors")[0]


def local(tile_values, tile_row, tile_col, tile_count, user_degree, item_degree, start_vectors):
    vectors, item_rows = start_vectors.shape
    slot_count, tile, _ = tile_values.shape
    user_rows = user_degree.shape[0]
    user_blocks = user_rows // tile
    item_blocks = item_rows // tile
    narrow_count = lax.axis_size("narrow")
    near_count = lax.axis_size("y") * lax.axis_size("z_low")
    all_users = user_rows * near_count * lax.axis_size("z_high")
    all_items = item_rows * narrow_count
    users = user_degree.reshape(user_blocks, 1, tile)
    items = item_degree.reshape(item_blocks, 1, tile)

    item_data = start_vectors
    for step in range(ITERS):
        first, last = step == 0, step == ITERS - 1
        (terms,) = phase(
            item_data, None if first else near_count, items, tile_values, tile_col, tile_row, tile_count, user_blocks, narrow_count, True,
            None if first else all_users, not first, False,
        )
        user_data = narrow_sum(terms)
        out = phase(
            user_data, narrow_count, users, tile_values, tile_row, tile_col, tile_count, item_blocks, near_count, False,
            None if first else all_items, True, last,
        )
        item_data = wide_sum(out[0])
    user_raw = out[1]
    item_raw, grams, user_inverse = finish_items(item_data, near_count, items, all_users, narrow_count)
    grams = exchange(grams, "narrow", narrow_count)
    user_vectors = finish_users(user_raw, user_inverse)
    item_vectors = finish_vectors(item_raw, grams, all_items)
    return (user_vectors, item_vectors)


def solution(mesh):
    wide_count, narrow_count = mesh.devices.shape
    grid = mesh.devices.reshape(Y_CHIPS, wide_count // (Y_CHIPS * Z_PAIR), Z_PAIR, narrow_count)
    wide = ("y", "z_high", "z_low")
    owner = wide + ("narrow",)
    return jax.shard_map(
        local,
        mesh=Mesh(grid, owner),
        in_specs=(
            P(owner, None, None),
            P(owner),
            P(owner),
            P(owner),
            P(wide),
            P("narrow"),
            P(None, "narrow"),
        ),
        out_specs=(P(None, wide), P(None, "narrow")),
        check_vma=False,
    )
```

```python
import math

import jax
import jax.numpy as jnp
from jax import lax
from jax.experimental import pallas as pl
from jax.experimental.pallas import tpu as pltpu
from jax.sharding import Mesh, PartitionSpec as P

ITERS = 2
GROUP = 128
BEGIN_GROUP = 64
Y_CHIPS = 8
Z_PAIR = 2
SUB = 8
WIDTH = 4
VMEM_LIMIT = 16 * 1024 * 1024
BEGIN_LIMIT = 57 * 1024 * 1024
FULL = lax.Precision.HIGHEST
VMEM = pl.BlockSpec(memory_space=pltpu.VMEM)
SMEM = pl.BlockSpec(memory_space=pltpu.SMEM)


def dot(a, b, last=False):
    dims = (((1,), (1,)), ((), ())) if last else (((1,), (0,)), ((), ()))
    return lax.dot_general(a, b, dims, precision=FULL, preferred_element_type=jnp.float32)


def inverse_factor(panels):
    vectors = len(panels) * SUB
    lane = lax.broadcasted_iota(jnp.int32, (SUB, 2 * vectors), 1)
    sub = lax.broadcasted_iota(jnp.int32, (SUB, 2 * vectors), 0)
    rows = []
    for p, panel in enumerate(panels):
        unit = jnp.where(lane == vectors + p * SUB + sub, 1.0, 0.0)
        rows.append(jnp.where(lane < vectors, panel, unit))

    def spread(panel, p):
        return [jnp.broadcast_to(panel[:, p * SUB + q : p * SUB + q + 1], panel.shape) for q in range(SUB)]

    def row(value, q):
        return jnp.broadcast_to(value[q : q + 1, :], value.shape)

    for p in range(len(panels)):
        cols = spread(rows[p], p)
        pivots, heads, inverses = [], [], []
        scale = jnp.ones_like(rows[p])
        for q in range(SUB):
            head = row(rows[p], q)
            tops = [None if t < q else row(cols[t], q) for t in range(SUB)]
            inverse = 1.0 / tops[q]
            pivots.append(head)
            heads.append(tops)
            inverses.append(inverse)
            scale = jnp.where(sub == q, tops[q], scale)
            factor = jnp.where(sub > q, cols[q] * inverse, 0.0)
            rows[p] = rows[p] - factor * head
            for t in range(q + 1, SUB):
                cols[t] = cols[t] - factor * tops[t]
        for r in range(p + 1, len(panels)):
            cols = spread(rows[r], p)
            for q in range(SUB):
                factor = cols[q] * inverses[q]
                rows[r] = rows[r] - factor * pivots[q]
                for t in range(q + 1, SUB):
                    cols[t] = cols[t] - factor * heads[q][t]
        rows[p] = rows[p] * lax.rsqrt(scale)
    return jnp.concatenate(rows, axis=0)[:, vectors:]


def read_block(ref, block, vectors, per_chunk, stride):
    part = math.gcd(vectors, per_chunk)
    pieces = []
    for row in range(block * vectors, (block + 1) * vectors, part):
        at = row // per_chunk * stride + row % per_chunk
        pieces.append(ref[at : at + part, :])
    return pieces[0] if len(pieces) == 1 else jnp.concatenate(pieces, axis=0)


def write_block(ref, block, value, per_chunk, stride):
    vectors = value.shape[0]
    part = math.gcd(vectors, per_chunk)
    for begin in range(0, vectors, part):
        row = block * vectors + begin
        at = row // per_chunk * stride + row % per_chunk
        ref[at : at + part, :] = value[begin : begin + part]


def pack(gram):
    half = gram.shape[0] // 2
    return jnp.concatenate([gram[:half], gram[half:]], axis=1)


def unpacked_panels(packed):
    vectors = packed.shape[1] // 2
    turned = jnp.concatenate([packed[:, vectors:], packed[:, :vectors]], axis=1)
    return [half[at : at + SUB] for half in (packed, turned) for at in range(0, vectors // 2, SUB)]


def gram_panels(ref, chunks, per_chunk, vectors, count):
    part = vectors // 2 // chunks
    stride = per_chunk + part
    rows = [ref[c * stride + per_chunk : (c + 1) * stride, :] for c in range(chunks)]
    return unpacked_panels(jnp.concatenate(rows, axis=0) * (1.0 / count))


def scale_of(degree):
    return lax.rsqrt(degree.astype(jnp.float32))


def phase(data, chunks, degree, tiles, src, dst, used, blocks_out, out_chunks, forward, gram_count, send_gram, keep_raw):
    slots, tile, _ = tiles.shape
    blocks = degree.shape[0]
    begins = chunks is None
    vectors = data.shape[0] if begins else tile // 2
    per_chunk = None if begins else blocks * vectors // chunks
    stride = None if begins else data.shape[0] // chunks
    have_gram = gram_count is not None
    terms = 1 if begins else 2
    out_per = blocks_out * vectors // out_chunks
    gram_rows = vectors // 2 // out_chunks if send_gram else 0
    out_stride = out_per + gram_rows
    group_slots = BEGIN_GROUP if begins else GROUP
    dims = (((1,), (1,)), ((), ())) if forward else (((1,), (0,)), ((), ()))

    def body(src_ref, dst_ref, used_ref, data_ref, degree_ref, tiles_ref, out_ref, *rest):
        if begins:
            x_ref, sums_ref, data_here, degree_here, tiles_here, whole_sem, group_sem = rest

            def group_copy(step):
                rows = pl.ds(step * group_slots, group_slots)
                return pltpu.make_async_copy(tiles_ref.at[rows], tiles_here.at[rows], group_sem.at[step])

            copies = [
                pltpu.make_async_copy(degree_ref, degree_here, whole_sem.at[0]),
                pltpu.make_async_copy(data_ref, data_here, whole_sem.at[1]),
            ]
            for copy in copies + [group_copy(step) for step in range(slots // group_slots)]:
                copy.start()
            for copy in copies:
                copy.wait()
            product_phase(src_ref, dst_ref, used_ref, data_here, degree_here, tiles_here, out_ref, None, x_ref, sums_ref, group_copy)
        elif keep_raw:
            raw_ref, x_ref, sums_ref = rest
            product_phase(src_ref, dst_ref, used_ref, data_ref, degree_ref, tiles_ref, out_ref, raw_ref, x_ref, sums_ref, None)
        else:
            x_ref, sums_ref = rest
            product_phase(src_ref, dst_ref, used_ref, data_ref, degree_ref, tiles_ref, out_ref, None, x_ref, sums_ref, None)

    def product_phase(src_ref, dst_ref, used_ref, data_ref, degree_ref, tiles_ref, out_ref, raw_ref, x_ref, sums_ref, copy_of):
        sums_ref[...] = jnp.zeros_like(sums_ref)
        if have_gram:
            inverse = inverse_factor(gram_panels(data_ref, chunks, per_chunk, vectors, gram_count))
        gram = jnp.zeros((vectors, vectors), jnp.float32)
        for first in range(0, blocks, WIDTH):
            group = range(first, first + WIDTH)
            weight = jnp.concatenate([scale_of(degree_ref[block]) for block in group], axis=1)
            if begins:
                raw = data_ref[:, first * tile : (first + WIDTH) * tile]
            else:
                raw = jnp.concatenate([read_block(data_ref, block, vectors, per_chunk, stride) for block in group], axis=1)
                if have_gram:
                    raw = dot(inverse, raw)
                raw = raw * weight
            if send_gram:
                gram = gram + dot(raw, raw, last=True)
            source = raw * weight
            high = source.astype(jnp.bfloat16)
            if terms == 2:
                low = (source - high.astype(jnp.float32)).astype(jnp.bfloat16)
            for at, block in enumerate(group):
                lanes = slice(at * tile, (at + 1) * tile)
                x_ref[block, :vectors, :] = high[:, lanes]
                if terms == 2:
                    x_ref[block, vectors:, :] = low[:, lanes]
                if keep_raw:
                    raw_ref[block] = raw[:, lanes]
        if send_gram:
            packed = pack(gram)
            for c in range(out_chunks):
                at = c * out_stride + out_per
                out_ref[at : at + gram_rows, :] = packed[c * gram_rows : (c + 1) * gram_rows]

        @pl.loop(0, slots // group_slots)
        def _(step):
            if copy_of is not None:
                copy_of(step).wait()
            for slot in range(group_slots):
                at = step * group_slots + slot
                product = lax.dot_general(
                    x_ref[src_ref[at]], tiles_ref[at], dims, preferred_element_type=jnp.float32
                )
                if terms == 2:
                    product = product[:vectors] + product[vectors:]
                sums_ref[jnp.where(at < used_ref[0], dst_ref[at], blocks_out)] += product

        for block in range(blocks_out):
            write_block(out_ref, block, sums_ref[block], out_per, out_stride)

    out_shape = [jax.ShapeDtypeStruct((out_chunks * out_stride, tile), jnp.float32)]
    if keep_raw:
        out_shape.append(jax.ShapeDtypeStruct((blocks, vectors, tile), jnp.float32))
    scratch = [
        pltpu.VMEM((blocks, terms * vectors, tile), jnp.bfloat16),
        pltpu.VMEM((blocks_out + 1, vectors, tile), jnp.float32),
    ]
    if begins:
        scratch += [
            pltpu.VMEM(data.shape, data.dtype),
            pltpu.VMEM(degree.shape, degree.dtype),
            pltpu.VMEM(tiles.shape, tiles.dtype),
            pltpu.SemaphoreType.DMA((2,)),
            pltpu.SemaphoreType.DMA((slots // group_slots,)),
        ]
        return pl.pallas_call(
            body,
            grid_spec=pltpu.PrefetchScalarGridSpec(
                num_scalar_prefetch=3,
                grid=(1,),
                in_specs=[pl.BlockSpec(memory_space=pl.ANY)] * 3,
                out_specs=[VMEM],
                scratch_shapes=scratch,
            ),
            out_shape=out_shape,
            compiler_params=pltpu.CompilerParams(vmem_limit_bytes=BEGIN_LIMIT),
            name="forward_begin",
        )(src, dst, used, data, degree, tiles)
    return pl.pallas_call(
        body,
        in_specs=[SMEM] * 3 + [VMEM] * 3,
        out_specs=[VMEM] * len(out_shape),
        scratch_shapes=scratch,
        out_shape=out_shape,
        compiler_params=pltpu.CompilerParams(vmem_limit_bytes=VMEM_LIMIT),
        name="forward" if forward else "backward",
    )(src, dst, used, data, degree, tiles)


def call(body, inputs, shapes, name):
    return pl.pallas_call(
        body,
        in_specs=[VMEM] * len(inputs),
        out_specs=[VMEM] * len(shapes),
        out_shape=[jax.ShapeDtypeStruct(s, jnp.float32) for s in shapes],
        compiler_params=pltpu.CompilerParams(vmem_limit_bytes=VMEM_LIMIT),
        name=name,
    )(*inputs)


def exchange(data, axis, count):
    return lax.all_to_all(data.reshape(count, 1, -1), axis, 0, 0).reshape(data.shape)


def sum_copies(got, count, copies, rows, stride):
    step = got.shape[0] // count

    def body(got_ref, out_ref):
        mine = got_ref[:rows, :]
        for c in range(1, count):
            mine = mine + got_ref[c * step : c * step + rows, :]
        if stride > rows:
            mine = jnp.concatenate([mine, jnp.zeros((stride - rows, mine.shape[1]), jnp.float32)], axis=0)
        for c in range(copies):
            out_ref[c * stride : (c + 1) * stride, :] = mine

    return call(body, [got], [(copies * stride, got.shape[1])], "sum_copies")[0]


def narrow_sum(data):
    count = lax.axis_size("narrow")
    rows = data.shape[0] // count
    return exchange(sum_copies(exchange(data, "narrow", count), count, count, rows, rows), "narrow", count)


def wide_sum(data):
    near = ("y", "z_low")
    near_count, far_count = lax.axis_size("y") * lax.axis_size("z_low"), lax.axis_size("z_high")
    rows = data.shape[0] // near_count
    stride = -(-rows // SUB) * SUB
    part = sum_copies(exchange(data, near, near_count), near_count, far_count, rows, stride)
    back = sum_copies(exchange(part, "z_high", far_count), far_count, near_count, rows, rows)
    return exchange(back, near, near_count)


def finish_items(data, chunks, degree, user_count, copies):
    rows, tile = data.shape
    blocks = degree.shape[0]
    vectors = tile // 2
    per_chunk = blocks * vectors // chunks
    stride = rows // chunks

    def body(data_ref, degree_ref, raw_ref, gram_ref, inverse_ref):
        inverse = inverse_factor(gram_panels(data_ref, chunks, per_chunk, vectors, user_count))
        inverse_ref[...] = inverse
        gram = jnp.zeros((vectors, vectors), jnp.float32)
        for first in range(0, blocks, WIDTH):
            group = range(first, first + WIDTH)
            weight = jnp.concatenate([scale_of(degree_ref[block]) for block in group], axis=1)
            raw = jnp.concatenate([read_block(data_ref, block, vectors, per_chunk, stride) for block in group], axis=1)
            raw = dot(inverse, raw) * weight
            gram = gram + dot(raw, raw, last=True)
            raw_ref[:, first * tile : (first + WIDTH) * tile] = raw
        packed = pack(gram)
        for c in range(copies):
            gram_ref[c * vectors // 2 : (c + 1) * vectors // 2, :] = packed

    shapes = [(vectors, blocks * tile), (copies * vectors // 2, tile), (vectors, vectors)]
    return call(body, [data, degree], shapes, "finish_items")


def finish_users(raw, inverse):
    blocks, vectors, tile = raw.shape

    def body(raw_ref, inverse_ref, out_ref):
        for block in range(blocks):
            out_ref[:, block * tile : (block + 1) * tile] = dot(inverse_ref[...], raw_ref[block])

    return call(body, [raw, inverse], [(vectors, blocks * tile)], "finish_users")[0]


def finish_vectors(raw, grams, item_count):
    vectors, rows = raw.shape
    half = vectors // 2
    width = WIDTH * grams.shape[1]

    def body(raw_ref, grams_ref, out_ref):
        packed = grams_ref[:half, :]
        for at in range(half, grams.shape[0], half):
            packed = packed + grams_ref[at : at + half, :]
        inverse = inverse_factor(unpacked_panels(packed * (1.0 / item_count)))
        for begin in range(0, rows, width):
            out_ref[:, begin : begin + width] = dot(inverse, raw_ref[:, begin : begin + width])

    return call(body, [raw, grams], [raw.shape], "finish_vectors")[0]


def local(tile_values, tile_row, tile_col, tile_count, user_degree, item_degree, start_vectors):
    vectors, item_rows = start_vectors.shape
    slot_count, tile, _ = tile_values.shape
    user_rows = user_degree.shape[0]
    user_blocks = user_rows // tile
    item_blocks = item_rows // tile
    narrow_count = lax.axis_size("narrow")
    near_count = lax.axis_size("y") * lax.axis_size("z_low")
    all_users = user_rows * near_count * lax.axis_size("z_high")
    all_items = item_rows * narrow_count
    users = user_degree.reshape(user_blocks, 1, tile)
    items = item_degree.reshape(item_blocks, 1, tile)

    item_data = start_vectors
    for step in range(ITERS):
        first, last = step == 0, step == ITERS - 1
        (terms,) = phase(
            item_data, None if first else near_count, items, tile_values, tile_col, tile_row, tile_count, user_blocks, narrow_count, True,
            None if first else all_users, not first, False,
        )
        user_data = narrow_sum(terms)
        out = phase(
            user_data, narrow_count, users, tile_values, tile_row, tile_col, tile_count, item_blocks, near_count, False,
            None if first else all_items, True, last,
        )
        item_data = wide_sum(out[0])
    user_raw = out[1]
    item_raw, grams, user_inverse = finish_items(item_data, near_count, items, all_users, narrow_count)
    grams = exchange(grams, "narrow", narrow_count)
    user_vectors = finish_users(user_raw, user_inverse)
    item_vectors = finish_vectors(item_raw, grams, all_items)
    return (user_vectors, item_vectors)


def solution(mesh):
    wide_count, narrow_count = mesh.devices.shape
    grid = mesh.devices.reshape(Y_CHIPS, wide_count // (Y_CHIPS * Z_PAIR), Z_PAIR, narrow_count)
    wide = ("y", "z_high", "z_low")
    owner = wide + ("narrow",)
    return jax.shard_map(
        local,
        mesh=Mesh(grid, owner),
        in_specs=(
            P(owner, None, None),
            P(owner),
            P(owner),
            P(owner),
            P(wide),
            P("narrow"),
            P(None, "narrow"),
        ),
        out_specs=(P(None, wide), P(None, "narrow")),
        check_vma=False,
    )
```
